256 devices in a mesh: mem: 16 (over z, x_lo), tx: 8 (over y, core), ty: 2 (over x_hi).
Axes of the slice: x: 4 (x_hi: 2, x_lo: 2; x = x_hi * 2 + x_lo), y: 4, z: 8, core: 2. Of those that a mesh axis runs over, the one named last changes fastest.
Arguments:
- alpha: float32 [128, 4, 128, 64], P('mem', None, 'tx', 'ty'), may hold values from -6 to 6
- filter_rate: float32 [128, 64], P('tx', 'ty'), may hold values from 0.1 to 0.24
- block_list: int32 [8, 2, 32], P('tx', 'ty'), may hold values from 0 to 127, as said below
- interp_weights: float32 [8, 2, 32, 64, 256], P('tx', 'ty'), may hold values from -0.75 to 0.75
- perturbations: bfloat16 [128, 4, 4, 512, 256], P('mem', None, None, ('tx', 'ty')), may hold values from -1.5 to 1.5
- obs_cells: int32 [8, 2, 512], P('tx', 'ty'), may hold values from 0 to 8191
- obs_count: int32 [8, 2], P('tx', 'ty'), may hold values from 1 to 512, as said below
- departures: float32 [8, 2, 16, 512], P('tx', 'ty', 'mem'), may hold values from -6 to 6
- obs_weight: float32 [8, 2, 16, 512], P('tx', 'ty', 'mem'), may hold values from 0.25 to 2.5
Outputs:
- increment: float32 [16, 512, 256], P('mem', ('tx', 'ty'))
- weighted_departure: float32 [8, 2, 16, 512], P('tx', 'ty', 'mem')
- gradient: float32 [128, 4, 128, 64], P('mem', None, 'tx', 'ty')
The draws below stay inside these ranges and needn't reach their ends.
Inputs may be any that keep to these rules, and one draw needn't show every extreme that they name: `block_list`: entries name coarse blocks numbered as in the reference program, of any tile. Among the fine blocks of one tile, at most 2 distinct coarse blocks of any one tile are named; every tile names exactly 2 distinct blocks of its own. `obs_count`: some tile has all 512 slots in use in every draw.
All inputs are finite; a program needn't handle non-finite values.
Results may differ from the reference program's by a relative error of at most 0.0003.
Values sent between devices are 32-bit elements; how exact they have to be, the bound alone decides.
A program may use at most 64 MiB of HBM per device.

```python
import math
import jax
import jax.numpy as jnp
from jax import lax

LEV = 4
VARS = 4
CB = 8
CXC = 16
CYC = 32
SWEEPS = 4
CAP = 2
OBS = 512
MEMBERS = 128
TILES_X = 8
TILES_Y = 2
NCX = 128
NCY = 64
SLABS = 16
BLK_DEV = 8
FBLK_DEV = 32
BCELLS = 256
CELLS_DEV = 8192
FBLOCKS = 512
N_TX = 8
N_TY = 2


def draw_block_list(key, part):
    tile_count = TILES_X * TILES_Y
    score_key = jax.random.fold_in(key, 101)
    step_key = jax.random.fold_in(key, 102)
    column_key = jax.random.fold_in(key, 105)
    slot_key = jax.random.fold_in(key, 103)
    full_key = jax.random.fold_in(key, 104)
    scores = jax.random.randint(score_key, (tile_count, tile_count, BLK_DEV), 0, 1 << 20) * BLK_DEV + jnp.arange(BLK_DEV, dtype=jnp.int32)
    chosen = jnp.argsort(scores, axis=-1)[:, :, :CAP].astype(jnp.int32)
    tile_ids = jnp.arange(tile_count, dtype=jnp.int32)[:, None]
    fine_ids = jnp.arange(FBLK_DEV, dtype=jnp.int32)[None, :]
    row_of = tile_ids // TILES_Y
    steps_x = jax.random.randint(step_key, (tile_count, FBLK_DEV), -1, 2)
    columns = jax.random.randint(column_key, (tile_count, FBLK_DEV), 0, TILES_Y)
    owner_rows = jnp.clip(row_of + steps_x, 0, TILES_X - 1)
    owners = owner_rows * TILES_Y + columns
    slot_ids = jax.random.randint(slot_key, (tile_count, FBLK_DEV), 0, CAP)
    own_first = fine_ids < CAP
    owners = jnp.where(own_first, tile_ids, owners)
    slot_ids = jnp.where(own_first, fine_ids, slot_ids)
    full_tile = jax.random.randint(full_key, (), 0, tile_count)
    near_count = 3 * TILES_Y
    spread = (tile_ids == full_tile) & (fine_ids >= CAP) & (fine_ids < CAP + near_count * CAP)
    near_index = (fine_ids - CAP) // CAP
    near_rows = jnp.clip(row_of + near_index // TILES_Y - 1, 0, TILES_X - 1)
    near_owner = near_rows * TILES_Y + near_index % TILES_Y
    owners = jnp.where(spread, near_owner, owners)
    slot_ids = jnp.where(spread, (fine_ids - CAP) % CAP, slot_ids)
    far_start = CAP + near_count * CAP
    far_spread = (tile_ids == full_tile) & (fine_ids >= far_start) & (fine_ids < far_start + CAP)
    far_owner = (full_tile + tile_count // 2) % tile_count
    owners = jnp.where(far_spread, far_owner, owners)
    slot_ids = jnp.where(far_spread, fine_ids - far_start, slot_ids)
    local_ids = chosen[jnp.broadcast_to(tile_ids, owners.shape), owners, slot_ids]
    return (owners * BLK_DEV + local_ids).reshape(TILES_X, TILES_Y, FBLK_DEV).astype(jnp.int32)


def draw_obs_count(key, part):
    shift_key = jax.random.fold_in(key, 201)
    jitter_key = jax.random.fold_in(key, 202)
    full_key = jax.random.fold_in(key, 203)
    shifts = jax.random.randint(shift_key, (TILES_X, TILES_Y), 0, 4)
    ceilings = OBS // jnp.left_shift(jnp.ones_like(shifts), shifts)
    jitter = jax.random.randint(jitter_key, (TILES_X, TILES_Y), 0, jnp.maximum(ceilings // 2, 1))
    counts = jnp.maximum(ceilings - jitter, 1)
    full_tile = jax.random.randint(full_key, (), 0, TILES_X * TILES_Y)
    flat_ids = jnp.arange(TILES_X * TILES_Y, dtype=jnp.int32).reshape(TILES_X, TILES_Y)
    return jnp.where(flat_ids == full_tile, OBS, counts).astype(jnp.int32)


def set_ends(values, own_key, low, high):
    longest = values.shape.index(max(values.shape))
    spots = []
    for shift in (0, 1):
        where = [jax.random.randint(jax.random.fold_in(own_key, axis), (), 0, length) for axis, length in enumerate(values.shape)]
        where[longest] = (where[longest] + shift) % values.shape[longest]
        spots.append(tuple(where))
    return values.at[spots[0]].set(low).at[spots[1]].set(high)


def block_levels(rng, dims, cuts, least, top_value):
    loudness, own = 1.0, jax.random.fold_in(rng, 6)
    for axis_at, parts in cuts:
        draws = jnp.exp(jax.random.uniform(jax.random.fold_in(own, axis_at), (parts,), jnp.float32, least / len(cuts), top_value / len(cuts)))
        loudness = loudness * jnp.repeat(draws, dims[axis_at] // parts).reshape([-1 if axis == axis_at else 1 for axis in range(len(dims))])
    return loudness


def noise(rng, shape, scale, limit, split=(), kind=jnp.bfloat16):
    entries = scale * jax.random.normal(rng, shape, jnp.float32)
    if split:
        entries = entries * block_levels(rng, shape, split, -0.22, 0.18)
    return jnp.clip(entries, -limit, limit).astype(kind)


def setup_inputs(seed: int = 0) -> dict:
    keys = jax.random.split(jax.random.key(seed), 10)
    alpha = noise(keys[0], (MEMBERS, LEV, NCX, NCY), 1.0, 6.0, ((0, 16), (2, 8), (3, 2)), jnp.float32)
    filter_rate = jnp.clip(0.1 + 0.13999999 * jax.random.uniform(keys[1], (NCX, NCY), jnp.float32) ** block_levels(keys[1], (NCX, NCY), ((0, 8), (1, 2)), -0.2, 0.2), 0.1, 0.24)
    block_list = draw_block_list(jax.random.fold_in(keys[9], 71), 0)
    interp_weights = noise(keys[3], (TILES_X, TILES_Y, FBLK_DEV, CB * CB, BCELLS), (CB * CB) ** -0.5, 0.75, ((0, 8), (1, 2)), jnp.float32)
    perturbations = noise(keys[4], (MEMBERS, LEV, VARS, FBLOCKS, BCELLS), 0.25, 1.5, ((0, 16), (3, 16)))
    obs_cells = set_ends(jax.random.randint(keys[5], (TILES_X, TILES_Y, OBS), 0, CELLS_DEV), jax.random.fold_in(keys[5], 1), 0, CELLS_DEV - 1).astype(jnp.int32)
    obs_count = draw_obs_count(jax.random.fold_in(keys[9], 71), 0)
    departures = noise(keys[7], (TILES_X, TILES_Y, SLABS, OBS), 1.0, 6.0, ((0, 8), (1, 2), (2, 16)), jnp.float32)
    obs_weight = jnp.clip(jnp.exp(math.log(2.5) - 2.3025851 * jax.random.uniform(keys[8], (TILES_X, TILES_Y, SLABS, OBS), jnp.float32) ** block_levels(keys[8], (TILES_X, TILES_Y, SLABS, OBS), ((0, 8), (1, 2), (2, 16)), -0.2, 0.2)), 0.25, 2.5)
    return {"alpha": alpha, "filter_rate": filter_rate, "block_list": block_list, "interp_weights": interp_weights, "perturbations": perturbations, "obs_cells": obs_cells, "obs_count": obs_count, "departures": departures, "obs_weight": obs_weight}


exact_mode = lax.Precision.HIGHEST


def beside_sum(coarse):
    padded = jnp.pad(coarse, ((0, 0), (1, 1), (1, 1)))
    return padded[:, 2:, 1:-1] + padded[:, :-2, 1:-1] + padded[:, 1:-1, 2:] + padded[:, 1:-1, :-2]


def smooth(coarse, filter_coef):
    for sweep_no in range(SWEEPS):
        coarse = coarse + filter_coef * (beside_sum(coarse) - 4.0 * coarse)
    return coarse


def smooth_adjoint(coarse, filter_coef):
    for sweep_no in range(SWEEPS):
        scaled = filter_coef * coarse
        coarse = coarse + beside_sum(scaled) - 4.0 * scaled
    return coarse


def to_blocks(coarse):
    row_count = coarse.shape[0]
    arranged = coarse.reshape(row_count, N_TX, CXC // CB, CB, N_TY, CYC // CB, CB).transpose(1, 4, 2, 5, 0, 3, 6)
    return arranged.reshape(-1, row_count, CB * CB)


def from_blocks(blocks, row_count):
    arranged = blocks.reshape(N_TX, N_TY, CXC // CB, CYC // CB, row_count, CB, CB).transpose(4, 0, 2, 5, 1, 3, 6)
    return arranged.reshape(row_count, NCX, NCY)


def reference(alpha, filter_rate, block_list, interp_weights, perturbations, obs_cells, obs_count, departures, obs_weight):
    row_count = MEMBERS * LEV
    tile_count = N_TX * N_TY
    filter_coef = filter_rate[None]
    smoothed = smooth(alpha.reshape(row_count, NCX, NCY), filter_coef)
    blocks = to_blocks(smoothed)
    wanted = block_list.reshape(-1).astype(jnp.int32)
    weights = interp_weights.reshape(-1, CB * CB, BCELLS)
    fine_alpha = jnp.einsum("frk,fkc->rfc", blocks[wanted], weights, precision=exact_mode)
    fine_alpha = fine_alpha.reshape(MEMBERS, LEV, -1, BCELLS)
    pert_full = perturbations.astype(jnp.float32)
    increment = jnp.sum(fine_alpha[:, :, None] * pert_full, axis=0).reshape(SLABS, -1, BCELLS)
    flat_inc = increment.reshape(SLABS, tile_count, CELLS_DEV)
    obs_where = obs_cells.reshape(tile_count, OBS).astype(jnp.int32)
    observed = jnp.take_along_axis(flat_inc, obs_where[None], axis=2).transpose(1, 0, 2)
    in_use = jnp.arange(OBS, dtype=jnp.int32)[None, None, :] < obs_count.reshape(tile_count, 1, 1)
    weighted = jnp.where(in_use, obs_weight.reshape(tile_count, SLABS, OBS) * (observed - departures.reshape(tile_count, SLABS, OBS)), 0.0)
    tile_ids = jnp.arange(tile_count, dtype=jnp.int32)[:, None, None]
    slab_ids = jnp.arange(SLABS, dtype=jnp.int32)[None, :, None]
    forcing = jnp.zeros((tile_count, SLABS, CELLS_DEV), jnp.float32).at[tile_ids, slab_ids, obs_where[:, None, :]].add(weighted)
    forcing = forcing.transpose(1, 0, 2).reshape(LEV, VARS, -1, BCELLS)
    fine_gradient = jnp.sum(pert_full * forcing[None], axis=2)
    contrib = jnp.einsum("rfc,fkc->frk", fine_gradient.reshape(row_count, -1, BCELLS), weights, precision=exact_mode)
    summed = jnp.zeros_like(blocks).at[wanted].add(contrib)
    adjoint = smooth_adjoint(from_blocks(summed, row_count), filter_coef)
    gradient = alpha + adjoint.reshape(alpha.shape)
    return increment, weighted.reshape(N_TX, N_TY, SLABS, OBS), gradient
```

```python
import jax
import jax.numpy as jnp
from jax import lax
from jax.experimental import pallas as pl
from jax.experimental.pallas import tpu as pltpu
from jax.sharding import PartitionSpec as P

MESH = pl.DeviceIdType.MESH
F32, BF16, I32 = jnp.float32, jnp.bfloat16, jnp.int32

LEV = 4
VARS = 4
CB = 8
CXC = 16
CYC = 32
SWEEPS = 4
OBS = 512
ROWS = 32
GROUPS = ROWS // 8
FINE = 32
CELLS = 256
SLABS = 16
TILES = 16
N_MEM = 16
N_TX = 8
BLOCKS = 8
LANES = 128


def lane_of(*shape):
    return lax.broadcasted_iota(I32, shape, len(shape) - 1)


def turned(value, shift):
    if isinstance(shift, int):
        shift %= LANES
        if shift == 0:
            return value
    return pltpu.roll(value, shift, axis=value.ndim - 1)


def halves(value):
    high = value.astype(BF16)
    return high, (value - high.astype(F32)).astype(BF16)


def device_halo(tx, ty):
    below, above = lax.rem(tx + N_TX - 1, N_TX), lax.rem(tx + 1, N_TX)
    return ((below, ty), (above, ty), (below, 1 - ty), (above, 1 - ty), (tx, 1 - ty))


def packed_halo(planes, ty):
    lane = lane_of(8, LANES)
    first = sum(turned(planes[j], CYC * j) for j in range(SWEEPS))
    last = sum(turned(planes[CXC - SWEEPS + j], CYC * j) for j in range(SWEEPS))
    start = (CYC - SWEEPS) * (1 - ty)
    side = 0.0
    for x in range(CXC):
        shift = lax.rem(SWEEPS * x - start + LANES, LANES)
        side = side + jnp.where(lane >> 2 == x, turned(planes[x], shift), 0.0)
    return first, last, side


def with_halo(planes, halo, tx, ty):
    lane = lane_of(8, LANES)
    own = lane < CYC
    side = (lane >> 2) == jnp.where(ty == 0, CYC // 4, LANES // 4 - 1)
    corner = jnp.where(ty == 0, CYC, 3 * CYC)
    place = jnp.where(ty == 0, CYC, LANES - SWEEPS)

    def beyond(straight, across, there):
        made = []
        for j in range(SWEEPS):
            plane = jnp.where(own, turned(straight, -CYC * j), 0.0)
            shift = lax.rem(corner - CYC * j + LANES, LANES)
            plane = plane + jnp.where(side, turned(across, shift), 0.0)
            made.append(jnp.where(there, plane, 0.0))
        return made

    low = beyond(halo[1], halo[3], tx > 0)
    high = beyond(halo[0], halo[2], tx < N_TX - 1)
    middle = []
    for x in range(CXC):
        shift = lax.rem(place - SWEEPS * x + LANES, LANES)
        middle.append(planes[x] + jnp.where(side, turned(halo[4], shift), 0.0))
    return jnp.stack(low + middle + high)


def kernel(
    block_list,
    obs_count,
    alpha,
    filter_rate,
    obs_cells,
    departures,
    obs_weight,
    weights_hbm,
    perturb_hbm,
    increment,
    weighted_out,
    gradient,
    weights,
    perturb,
    split,
    rows,
    planes,
    rates,
    select,
    halo_out,
    halo_in,
    code_out,
    code_in,
    kept,
    blocks,
    block_out,
    block_in,
    fine_a,
    fine_b,
    slab,
    slab_in,
    weighted,
    cell_hot,
    spread,
    forcing,
    contrib,
    back_out,
    back_in,
    edge_out,
    edge_in,
    load_sem,
    halo_sem,
    code_sem,
    block_sem,
    slab_sem,
    weighted_sem,
    back_sem,
    edge_sem,
):
    mem, tx, ty = lax.axis_index("mem"), lax.axis_index("tx"), lax.axis_index("ty")
    tile = tx * 2 + ty
    lane = lane_of(8, LANES)

    load_weights = pltpu.make_async_copy(weights_hbm, weights, load_sem.at[0])
    load_perturb = pltpu.make_async_copy(perturb_hbm, perturb, load_sem.at[1])
    load_weights.start()
    load_perturb.start()

    def tile_at(i):
        return lax.rem(tile + i, TILES)

    def tile_device(t):
        return {"tx": t // 2, "ty": lax.rem(t, 2)}

    def mem_at(i):
        return lax.rem(mem + i, N_MEM)

    barrier = pltpu.get_barrier_semaphore()

    def greet(i, carry):
        pl.semaphore_signal(
            barrier, inc=1, device_id=tile_device(tile_at(i)), device_id_type=MESH
        )
        pl.semaphore_signal(
            barrier, inc=1, device_id={"mem": mem_at(i)}, device_id_type=MESH
        )
        return carry

    lax.fori_loop(1, TILES, greet, 0)

    def to_tile(src, dst, sem, t, slot):
        return pltpu.make_async_remote_copy(
            src_ref=src,
            dst_ref=dst,
            send_sem=sem.at[0, t],
            recv_sem=sem.at[1, slot],
            device_id=tile_device(t),
            device_id_type=MESH,
        )

    def to_member(src, dst, sem, m, slot):
        return pltpu.make_async_remote_copy(
            src_ref=src,
            dst_ref=dst,
            send_sem=sem.at[0, m],
            recv_sem=sem.at[1, slot],
            device_id={"mem": m},
            device_id_type=MESH,
        )

    def halo_copies(out, into, sem):
        sources = (0, 1, 0, 1, 2)
        return [
            pltpu.make_async_remote_copy(
                src_ref=out.at[sources[i]],
                dst_ref=into.at[i],
                send_sem=sem.at[0, i],
                recv_sem=sem.at[1, i],
                device_id={"tx": x, "ty": y},
                device_id_type=MESH,
            )
            for i, (x, y) in enumerate(device_halo(tx, ty))
        ]

    rows[...] = jnp.zeros_like(rows)
    rows[:, 0:CYC] = alpha[...]
    rates[...] = jnp.zeros_like(rates)
    for x in range(CXC):
        planes[x] = rows[pl.ds(x, ROWS, stride=CXC), :].reshape(GROUPS, 8, LANES)
        rates[SWEEPS + x, :, 0:CYC] = jnp.broadcast_to(
            filter_rate[x : x + 1, :], (8, CYC)
        )
    both = jnp.concatenate(
        [planes[...], rates[SWEEPS : SWEEPS + CXC][:, None]], axis=1
    )
    for i, message in enumerate(packed_halo(both, ty)):
        halo_out[i] = message

    asked = lane < 0
    for f in range(FINE):
        asked = asked | (lane == block_list[0, f])
    asked = jnp.where(asked, 1.0, 0.0)
    second = jnp.zeros((8, LANES), F32)
    for j in range(1, BLOCKS):
        second = jnp.maximum(second, jnp.where((lane & 7) >= j, turned(asked, j), 0.0))
    code_out[...] = asked * (1.0 + second)

    pl.semaphore_wait(barrier, 2 * (TILES - 1))
    first_halo = halo_copies(halo_out, halo_in, halo_sem)
    for copy in first_halo:
        copy.start()

    def send_code(i, carry):
        t = tile_at(i)
        to_tile(code_out, code_in.at[tile], code_sem, t, tile).start()
        return carry

    lax.fori_loop(1, TILES, send_code, 0)
    code_in[tile] = code_out[...]

    side_half = jnp.where(lane < 64, 0.0, 1.0)
    for f in range(FINE):
        wanted = block_list[0, f]
        rank = jnp.max(jnp.where(lane == wanted, second, 0.0), axis=1, keepdims=True)
        select[f] = jnp.where(side_half == rank, wanted >> 3, -1)

    cells = obs_cells[...]
    cell_hot[...] = jnp.where(
        lax.broadcasted_iota(I32, (CELLS, OBS), 0) == (cells & (CELLS - 1)), 1.0, 0.0
    ).astype(BF16)

    def wait_code(i, carry):
        t = tile_at(i)
        to_tile(code_out, code_in.at[t], code_sem, t, t).wait_recv()
        return carry

    lax.fori_loop(1, TILES, wait_code, 0)
    lane3 = lane_of(TILES, 8, LANES)
    mine = (lane3 >> 3) == tile
    local = (lane3 & 7).astype(F32)
    codes = code_in[...]
    slot_0 = jnp.sum(jnp.where(mine & (codes == 1.0), local, 0.0), axis=2, keepdims=True)
    slot_1 = jnp.sum(jnp.where(mine & (codes == 2.0), local, 0.0), axis=2, keepdims=True)
    kept[...] = jnp.where(lane3 < 64, slot_0, slot_1)

    for copy in first_halo:
        copy.wait_recv()

    whole = with_halo(both, halo_in, tx, ty)
    field, rate = whole[:, :GROUPS], whole[:, GROUPS:]
    rates[...] = rate[:, 0]
    for sweep in range(SWEEPS):
        center = field[1:-1]
        beside = field[2:] + field[:-2] + turned(center, 1) + turned(center, -1)
        field = center + rate[1 + sweep : 23 - sweep] * (beside - 4.0 * center)

    field = jnp.where(lane < CYC, field, 0.0)
    field = (field + turned(field, 64)).reshape(2, CB, GROUPS, 8, LANES)
    for ky in range(CYC // CB):
        block = 0.0
        for x in range(CB):
            block = block + jnp.where(
                ((lane & 63) >> 3) == x, turned(field[:, x], CB * (x - ky)), 0.0
            )
        for kx in range(2):
            blocks[kx * (CYC // CB) + ky] = block[kx]

    def chosen(t):
        number = kept[t]
        block = jnp.zeros((GROUPS, 8, LANES), F32)
        for k in range(BLOCKS):
            block = jnp.where(number == float(k), blocks[k], block)
        return block

    def send_blocks(i, carry):
        t = tile_at(i)
        block_out[t] = chosen(t)
        to_tile(block_out.at[t], block_in.at[tile], block_sem, t, tile).start()
        return carry

    lax.fori_loop(1, TILES, send_blocks, 0)
    block_in[tile] = chosen(tile)

    load_weights.wait()

    def split_weights(f, carry):
        high, low = halves(weights[f])
        split[f, 0:64] = high
        split[f, 64:128] = low
        return carry

    lax.fori_loop(0, FINE, split_weights, 0)
    load_perturb.wait()

    def wait_blocks(i, carry):
        t = tile_at(i)
        to_tile(block_out.at[t], block_in.at[t], block_sem, t, t).wait_recv()
        return carry

    lax.fori_loop(1, TILES, wait_blocks, 0)

    for f in range(FINE):
        value = block_in[block_list[0, f] >> 3]
        value = jnp.where(select[f] >= 0, value, turned(value, 64))
        high, low = halves(value.reshape(ROWS, LANES))
        product = jnp.dot(
            jnp.concatenate([high, low], axis=0), split[f], preferred_element_type=F32
        )
        product = product[:ROWS] + product[ROWS:]
        fine_a[pl.ds(f, ROWS, stride=FINE), :] = product[:, :LANES]
        fine_b[pl.ds(f, ROWS, stride=FINE), :] = product[:, LANES:]

    def share(i, carry):
        level = lax.rem(mem // VARS + 1 + i, LEV)
        for half, fine in enumerate((fine_a, fine_b)):
            sums = [jnp.zeros((FINE, LANES), F32)] * VARS
            for m in range(ROWS // LEV):
                row = m * LEV + level
                value = fine[pl.ds(pl.multiple_of(row * FINE, FINE), FINE), :]
                for v in range(VARS):
                    part = perturb[row * VARS + v, :, half * LANES : (half + 1) * LANES]
                    sums[v] = sums[v] + value * part.astype(F32)
            for v in range(VARS):
                slab[level * VARS + v, :, half * LANES : (half + 1) * LANES] = sums[v]
        for v in range(VARS):
            s = level * VARS + v

            @pl.when(s != mem)
            def _():
                to_member(slab.at[s], slab_in.at[mem], slab_sem, s, mem).start()

        return carry

    lax.fori_loop(0, LEV, share, 0)

    def gather_slab(i, total):
        m = mem_at(i)
        to_member(slab.at[m], slab_in.at[m], slab_sem, m, m).wait_recv()
        return total + slab_in[m]

    total = lax.fori_loop(1, N_MEM, gather_slab, slab[mem])
    increment[...] = total

    fine_of = (cells >> 8) == lax.broadcasted_iota(I32, (FINE, OBS), 0)
    high, low = halves(total)
    at_cells = jnp.dot(
        jnp.concatenate([high, low], axis=0), cell_hot[...], preferred_element_type=F32
    )
    at_cells = at_cells[:FINE] + at_cells[FINE:]
    observed = jnp.sum(jnp.where(fine_of, at_cells, 0.0), axis=0, keepdims=True)
    in_use = lane_of(1, OBS) < obs_count[0, 0]
    residual = jnp.where(in_use, obs_weight[...] * (observed - departures[...]), 0.0)
    weighted_out[...] = residual
    weighted[mem] = residual

    def send_weighted(i, carry):
        m = mem_at(i)
        to_member(weighted.at[mem], weighted.at[mem], weighted_sem, m, mem).start()
        return carry

    lax.fori_loop(1, N_MEM, send_weighted, 0)

    def wait_weighted(i, carry):
        m = mem_at(i)
        to_member(weighted.at[m], weighted.at[m], weighted_sem, m, m).wait_recv()
        return carry

    lax.fori_loop(1, N_MEM, wait_weighted, 0)

    for s in range(SLABS):
        high, low = halves(weighted[s])
        spread[s * FINE : (s + 1) * FINE, :] = jnp.where(
            fine_of, high.astype(F32), 0.0
        ).astype(BF16)
        spread[(SLABS + s) * FINE : (SLABS + s + 1) * FINE, :] = jnp.where(
            fine_of, low.astype(F32), 0.0
        ).astype(BF16)
    forced = lax.dot_general(
        spread[...],
        cell_hot[...],
        (((1,), (1,)), ((), ())),
        preferred_element_type=F32,
    )
    forced = forced[: SLABS * FINE] + forced[SLABS * FINE :]
    forcing[...] = forced.reshape(SLABS, FINE, CELLS)

    def fine_gradient(level, carry):
        for half, fine in enumerate((fine_a, fine_b)):
            cut = slice(half * LANES, (half + 1) * LANES)
            parts = [forcing[level * VARS + v, :, cut] for v in range(VARS)]
            for m in range(ROWS // LEV):
                row = m * LEV + level
                value = sum(
                    perturb[row * VARS + v, :, cut].astype(F32) * parts[v]
                    for v in range(VARS)
                )
                fine[pl.ds(pl.multiple_of(row * FINE, FINE), FINE), :] = value
        return carry

    lax.fori_loop(0, LEV, fine_gradient, 0)

    for f in range(FINE):
        value = jnp.concatenate(
            [
                fine_a[pl.ds(f, ROWS, stride=FINE), :],
                fine_b[pl.ds(f, ROWS, stride=FINE), :],
            ],
            axis=1,
        )
        high, low = halves(value)
        product = lax.dot_general(
            jnp.concatenate([high, low], axis=0),
            split[f],
            (((1,), (1,)), ((), ())),
            preferred_element_type=F32,
        )
        product = product[:ROWS] + product[ROWS:]
        product = product + turned(product, 64)
        contrib[f] = product.reshape(GROUPS, 8, LANES)

    def returned(t):
        block = jnp.zeros((GROUPS, 8, LANES), F32)
        for f in range(FINE):
            block = block + jnp.where(select[f] == t, contrib[f], 0.0)
        return block

    def send_back(i, carry):
        t = tile_at(i)
        back_out[t] = returned(t)
        to_tile(back_out.at[t], back_in.at[tile], back_sem, t, tile).start()
        return carry

    lax.fori_loop(1, TILES, send_back, 0)
    back_in[tile] = returned(tile)

    def wait_back(i, carry):
        t = tile_at(i)
        to_tile(back_out.at[t], back_in.at[t], back_sem, t, t).wait_recv()
        return carry

    lax.fori_loop(1, TILES, wait_back, 0)

    for k in range(BLOCKS):
        block = jnp.zeros((GROUPS, 8, LANES), F32)
        for t in range(TILES):
            block = block + jnp.where(kept[t] == float(k), back_in[t], 0.0)
        blocks[k] = block + turned(block, 64)

    coarse = []
    for x in range(CXC):
        plane = 0.0
        for ky in range(CYC // CB):
            plane = plane + jnp.where(
                (lane >> 3) == ky,
                turned(blocks[x // CB * (CYC // CB) + ky], CB * (ky - x % CB)),
                0.0,
            )
        coarse.append(plane)
    for i, message in enumerate(packed_halo(coarse, ty)):
        edge_out[i] = message
    second_halo = halo_copies(edge_out, edge_in, edge_sem)
    for copy in second_halo:
        copy.start()
    for copy in second_halo:
        copy.wait_recv()
    field = with_halo(coarse, edge_in, tx, ty)
    rate = rates[...][:, None]
    for sweep in range(SWEEPS):
        scaled = rate[sweep : 24 - sweep] * field
        inner = scaled[1:-1]
        beside = scaled[2:] + scaled[:-2] + turned(inner, 1) + turned(inner, -1)
        field = field[1:-1] + beside - 4.0 * inner
    field = field + planes[...]
    for x in range(CXC):
        rows[pl.ds(x, ROWS, stride=CXC), :] = field[x].reshape(ROWS, LANES)
    gradient[...] = rows[:, 0:CYC]

    for copy in first_halo + second_halo:
        copy.wait_send()

    def wait_sent(i, carry):
        t, m = tile_at(i), mem_at(i)
        to_tile(code_out, code_in.at[tile], code_sem, t, tile).wait_send()
        to_tile(block_out.at[t], block_in.at[tile], block_sem, t, tile).wait_send()
        to_tile(back_out.at[t], back_in.at[tile], back_sem, t, tile).wait_send()
        to_member(slab.at[m], slab_in.at[mem], slab_sem, m, mem).wait_send()
        to_member(weighted.at[mem], weighted.at[mem], weighted_sem, m, mem).wait_send()
        return carry

    lax.fori_loop(1, TILES, wait_sent, 0)


def on_device(
    alpha,
    filter_rate,
    block_list,
    interp_weights,
    perturbations,
    obs_cells,
    obs_count,
    departures,
    obs_weight,
):
    in_vmem = pl.BlockSpec(memory_space=pltpu.VMEM)
    in_smem = pl.BlockSpec(memory_space=pltpu.SMEM)
    anywhere = pl.BlockSpec(memory_space=pl.ANY)
    dma = pltpu.SemaphoreType.DMA
    increment, weighted, gradient = pl.pallas_call(
        kernel,
        out_shape=(
            jax.ShapeDtypeStruct((FINE, CELLS), F32),
            jax.ShapeDtypeStruct((1, OBS), F32),
            jax.ShapeDtypeStruct((ROWS * CXC, CYC), F32),
        ),
        in_specs=[in_smem] * 2 + [in_vmem] * 5 + [anywhere] * 2,
        out_specs=(in_vmem,) * 3,
        scratch_shapes=[
            pltpu.VMEM((FINE, 64, CELLS), F32),
            pltpu.VMEM((ROWS * VARS, FINE, CELLS), BF16),
            pltpu.VMEM((FINE, 128, CELLS), BF16),
            pltpu.VMEM((ROWS * CXC, LANES), F32),
            pltpu.VMEM((CXC, GROUPS, 8, LANES), F32),
            pltpu.VMEM((CXC + 2 * SWEEPS, 8, LANES), F32),
            pltpu.VMEM((FINE, 8, LANES), I32),
            pltpu.VMEM((3, GROUPS + 1, 8, LANES), F32),
            pltpu.VMEM((5, GROUPS + 1, 8, LANES), F32),
            pltpu.VMEM((8, LANES), F32),
            pltpu.VMEM((TILES, 8, LANES), F32),
            pltpu.VMEM((TILES, 8, LANES), F32),
            pltpu.VMEM((BLOCKS, GROUPS, 8, LANES), F32),
            pltpu.VMEM((TILES, GROUPS, 8, LANES), F32),
            pltpu.VMEM((TILES, GROUPS, 8, LANES), F32),
            pltpu.VMEM((ROWS * FINE, LANES), F32),
            pltpu.VMEM((ROWS * FINE, LANES), F32),
            pltpu.VMEM((SLABS, FINE, CELLS), F32),
            pltpu.VMEM((SLABS, FINE, CELLS), F32),
            pltpu.VMEM((SLABS, 1, OBS), F32),
            pltpu.VMEM((CELLS, OBS), BF16),
            pltpu.VMEM((2 * SLABS * FINE, OBS), BF16),
            pltpu.VMEM((SLABS, FINE, CELLS), F32),
            pltpu.VMEM((FINE, GROUPS, 8, LANES), F32),
            pltpu.VMEM((TILES, GROUPS, 8, LANES), F32),
            pltpu.VMEM((TILES, GROUPS, 8, LANES), F32),
            pltpu.VMEM((3, GROUPS, 8, LANES), F32),
            pltpu.VMEM((5, GROUPS, 8, LANES), F32),
            dma((2,)),
            dma((2, 5)),
            dma((2, TILES)),
            dma((2, TILES)),
            dma((2, N_MEM)),
            dma((2, N_MEM)),
            dma((2, TILES)),
            dma((2, 5)),
        ],
        compiler_params=pltpu.CompilerParams(
            collective_id=0, has_side_effects=True, vmem_limit_bytes=40 << 20
        ),
    )(
        block_list.reshape(1, FINE),
        obs_count.reshape(1, 1),
        alpha.reshape(ROWS * CXC, CYC),
        filter_rate,
        obs_cells.reshape(1, OBS),
        departures.reshape(1, OBS),
        obs_weight.reshape(1, OBS),
        interp_weights.reshape(FINE, 64, CELLS),
        perturbations.reshape(ROWS * VARS, FINE, CELLS),
    )
    return (
        increment.reshape(1, FINE, CELLS),
        weighted.reshape(departures.shape),
        gradient.reshape(alpha.shape),
    )


def solution(mesh):
    return jax.shard_map(
        on_device,
        mesh=mesh,
        in_specs=(
            P("mem", None, "tx", "ty"),
            P("tx", "ty"),
            P("tx", "ty", None),
            P("tx", "ty", None, None, None),
            P("mem", None, None, ("tx", "ty"), None),
            P("tx", "ty", None),
            P("tx", "ty"),
            P("tx", "ty", "mem", None),
            P("tx", "ty", "mem", None),
        ),
        out_specs=(
            P("mem", ("tx", "ty"), None),
            P("tx", "ty", "mem", None),
            P("mem", None, "tx", "ty"),
        ),
        check_vma=False,
    )
```

```python
import jax
import jax.numpy as jnp
from jax import lax
from jax.experimental import pallas as pl
from jax.experimental.pallas import tpu as pltpu
from jax.sharding import PartitionSpec as P

MESH = pl.DeviceIdType.MESH
F32, BF16, I32 = jnp.float32, jnp.bfloat16, jnp.int32

LEV = 4
VARS = 4
CB = 8
CXC = 16
CYC = 32
SWEEPS = 4
OBS = 512
ROWS = 32
GROUPS = ROWS // 8
FINE = 32
CELLS = 256
SLABS = 16
TILES = 16
N_MEM = 16
N_TX = 8
BLOCKS = 8
LANES = 128


def lane_of(*shape):
    return lax.broadcasted_iota(I32, shape, len(shape) - 1)


def turned(value, shift):
    if isinstance(shift, int):
        shift %= LANES
        if shift == 0:
            return value
    return pltpu.roll(value, shift, axis=value.ndim - 1)


def halves(value):
    high = value.astype(BF16)
    return high, (value - high.astype(F32)).astype(BF16)


def device_halo(tx, ty):
    below, above = lax.rem(tx + N_TX - 1, N_TX), lax.rem(tx + 1, N_TX)
    return ((below, ty), (above, ty), (below, 1 - ty), (above, 1 - ty), (tx, 1 - ty))


def packed_halo(planes, ty):
    lane = lane_of(8, LANES)
    first = sum(turned(planes[j], CYC * j) for j in range(SWEEPS))
    last = sum(turned(planes[CXC - SWEEPS + j], CYC * j) for j in range(SWEEPS))
    start = (CYC - SWEEPS) * (1 - ty)
    side = 0.0
    for x in range(CXC):
        shift = lax.rem(SWEEPS * x - start + LANES, LANES)
        side = side + jnp.where(lane >> 2 == x, turned(planes[x], shift), 0.0)
    return first, last, side


def with_halo(planes, halo, tx, ty):
    lane = lane_of(8, LANES)
    own = lane < CYC
    side = (lane >> 2) == jnp.where(ty == 0, CYC // 4, LANES // 4 - 1)
    corner = jnp.where(ty == 0, CYC, 3 * CYC)
    place = jnp.where(ty == 0, CYC, LANES - SWEEPS)

    def beyond(straight, across, there):
        made = []
        for j in range(SWEEPS):
            plane = jnp.where(own, turned(straight, -CYC * j), 0.0)
            shift = lax.rem(corner - CYC * j + LANES, LANES)
            plane = plane + jnp.where(side, turned(across, shift), 0.0)
            made.append(jnp.where(there, plane, 0.0))
        return made

    low = beyond(halo[1], halo[3], tx > 0)
    high = beyond(halo[0], halo[2], tx < N_TX - 1)
    middle = []
    for x in range(CXC):
        shift = lax.rem(place - SWEEPS * x + LANES, LANES)
        middle.append(planes[x] + jnp.where(side, turned(halo[4], shift), 0.0))
    return jnp.stack(low + middle + high)


def kernel(
    block_list_hbm,
    obs_count_hbm,
    alpha_hbm,
    filter_rate_hbm,
    obs_cells_hbm,
    departures_hbm,
    obs_weight_hbm,
    weights_hbm,
    perturb_hbm,
    increment,
    weighted_out,
    gradient,
    block_list,
    obs_count,
    alpha,
    filter_rate,
    obs_cells,
    departures,
    obs_weight,
    weights,
    perturb,
    split,
    rows,
    planes,
    rates,
    select,
    halo_out,
    halo_in,
    code_out,
    code_in,
    kept,
    blocks,
    block_out,
    block_in,
    fine_a,
    fine_b,
    slab,
    slab_in,
    weighted,
    seen_out,
    seen_in,
    cell_tall,
    cell_wide,
    spread,
    forcing,
    contrib,
    back_out,
    back_in,
    edge_out,
    edge_in,
    load_sem,
    halo_sem,
    code_sem,
    block_sem,
    slab_sem,
    weighted_sem,
    seen_sem,
    back_sem,
    edge_sem,
    news,
):
    mem, tx, ty = lax.axis_index("mem"), lax.axis_index("tx"), lax.axis_index("ty")
    tile = tx * 2 + ty
    lane = lane_of(8, LANES)
    sent = []

    loads = [
        pltpu.make_async_copy(source, target, load_sem.at[i])
        for i, (source, target) in enumerate(
            (
                (alpha_hbm, alpha),
                (filter_rate_hbm, filter_rate),
                (block_list_hbm, block_list),
                (obs_count_hbm, obs_count),
                (obs_cells_hbm, obs_cells),
                (departures_hbm, departures),
                (obs_weight_hbm, obs_weight),
                (weights_hbm, weights),
                (perturb_hbm, perturb),
            )
        )
    ]
    for load in loads:
        load.start()
    load_weights, load_perturb = loads[7:]

    y, core = lax.div(tx, 2), lax.rem(tx, 2)
    z, run = lax.div(mem, 2), lax.rem(mem, 2)

    def tile_by(dy, dcore, dty):
        to_core = 1 - core if dcore else core
        return (lax.rem(y + dy, 4) * 2 + to_core) * 2 + (1 - ty if dty else ty)

    def mem_by(dz, drun):
        return lax.rem(z + dz, 8) * 2 + (1 - run if drun else run)

    other_tiles = [
        tile_by(dy, dcore, dty) for dty in (1, 0) for dy in (2, 1, 3, 0) for dcore in (1, 0)
    ][:-1]
    other_mems = [
        mem_by(dz, drun) for dz in (4, 3, 5, 2, 6, 1, 7, 0) for drun in (1, 0)
    ][:-1]

    def tile_at(i):
        return lax.rem(tile + i, TILES)

    def tile_device(t):
        return {"tx": lax.div(t, 2), "ty": lax.rem(t, 2)}

    def mem_at(i):
        return lax.rem(mem + i, N_MEM)

    beside_mems = [mem_by(1, 0), mem_by(7, 0), mem_by(0, 1)]
    two_off_mems = [mem_by(2, 0), mem_by(6, 0), mem_by(0, 1)]
    barrier = pltpu.get_barrier_semaphore()
    for t in other_tiles:
        pl.semaphore_signal(
            barrier, inc=1, device_id=tile_device(t), device_id_type=MESH
        )
    for m in beside_mems:
        pl.semaphore_signal(barrier, inc=1, device_id={"mem": m}, device_id_type=MESH)

    def tell(step, members):
        for m in members:
            pl.semaphore_signal(
                news.at[step], inc=1, device_id={"mem": m}, device_id_type=MESH
            )

    def to_tile(src, dst, sem, t, slot):
        return pltpu.make_async_remote_copy(
            src_ref=src,
            dst_ref=dst,
            send_sem=sem.at[0, t],
            recv_sem=sem.at[1, slot],
            device_id=tile_device(t),
            device_id_type=MESH,
        )

    def to_member(src, dst, sem, m, slot):
        return pltpu.make_async_remote_copy(
            src_ref=src,
            dst_ref=dst,
            send_sem=sem.at[0, m],
            recv_sem=sem.at[1, slot],
            device_id={"mem": m},
            device_id_type=MESH,
        )

    def halo_copies(out, into, sem):
        sources = (0, 1, 0, 1, 2)
        return [
            pltpu.make_async_remote_copy(
                src_ref=out.at[sources[i]],
                dst_ref=into.at[i],
                send_sem=sem.at[0, i],
                recv_sem=sem.at[1, i],
                device_id={"tx": x, "ty": y},
                device_id_type=MESH,
            )
            for i, (x, y) in enumerate(device_halo(tx, ty))
        ]

    rows[...] = jnp.zeros_like(rows)
    rates[...] = jnp.zeros_like(rates)
    for load in loads[:7]:
        load.wait()
    rows[:, 0:CYC] = alpha[...]
    for x in range(CXC):
        planes[x] = rows[pl.ds(x, ROWS, stride=CXC), :].reshape(GROUPS, 8, LANES)
        rates[SWEEPS + x, :, 0:CYC] = jnp.broadcast_to(
            filter_rate[x : x + 1, :], (8, CYC)
        )
    both = jnp.concatenate(
        [planes[...], rates[SWEEPS : SWEEPS + CXC][:, None]], axis=1
    )
    for i, message in enumerate(packed_halo(both, ty)):
        halo_out[i] = message

    asked = lane < 0
    for f in range(FINE):
        asked = asked | (lane == block_list[0, f])
    asked = jnp.where(asked, 1.0, 0.0)
    second = jnp.zeros((8, LANES), F32)
    for j in range(1, BLOCKS):
        second = jnp.maximum(second, jnp.where((lane & 7) >= j, turned(asked, j), 0.0))
    code_out[...] = asked * (1.0 + second)

    pl.semaphore_wait(barrier, TILES - 1 + 3)
    first_halo = halo_copies(halo_out, halo_in, halo_sem)
    for t in other_tiles[:6]:
        to_tile(code_out, code_in.at[tile], code_sem, t, tile).start()
    for copy in first_halo:
        copy.start()
    for t in other_tiles[6:]:
        to_tile(code_out, code_in.at[tile], code_sem, t, tile).start()
    tell(0, beside_mems)
    sent.append(lambda i: to_tile(code_out, code_in.at[tile], code_sem, tile_at(i), tile))
    code_in[tile] = code_out[...]

    side_half = jnp.where(lane < 64, 0.0, 1.0)
    for f in range(FINE):
        wanted = block_list[0, f]
        rank = jnp.max(jnp.where(lane == wanted, second, 0.0), axis=1, keepdims=True)
        select[f] = jnp.where(side_half == rank, wanted >> 3, -1)

    cells = obs_cells[...]
    cell_hot = jnp.where(
        lax.broadcasted_iota(I32, (CELLS, OBS), 0) == (cells & (CELLS - 1)), 1.0, 0.0
    ).astype(BF16)
    for i in range(2):
        cell_tall[i * CELLS : (i + 1) * CELLS, :] = cell_hot
        cell_wide[:, i * OBS : (i + 1) * OBS] = cell_hot

    def wait_code(i, carry):
        t = tile_at(i)
        to_tile(code_out, code_in.at[t], code_sem, t, t).wait_recv()
        return carry

    lax.fori_loop(1, TILES, wait_code, 0)
    lane3 = lane_of(TILES, 8, LANES)
    mine = (lane3 >> 3) == tile
    local = (lane3 & 7).astype(F32)
    codes = code_in[...]
    slot_0 = jnp.sum(jnp.where(mine & (codes == 1.0), local, 0.0), axis=2, keepdims=True)
    slot_1 = jnp.sum(jnp.where(mine & (codes == 2.0), local, 0.0), axis=2, keepdims=True)
    kept[...] = jnp.where(lane3 < 64, slot_0, slot_1)

    for copy in first_halo:
        copy.wait_recv()
    pl.semaphore_wait(news.at[0], 3)
    tell(1, two_off_mems)

    whole = with_halo(both, halo_in, tx, ty)
    field, rate = whole[:, :GROUPS], whole[:, GROUPS:]
    rates[...] = rate[:, 0]
    for sweep in range(SWEEPS):
        center = field[1:-1]
        beside = field[2:] + field[:-2] + turned(center, 1) + turned(center, -1)
        field = center + rate[1 + sweep : 23 - sweep] * (beside - 4.0 * center)

    field = jnp.where(lane < CYC, field, 0.0)
    field = (field + turned(field, 64)).reshape(2, CB, GROUPS, 8, LANES)
    for ky in range(CYC // CB):
        block = 0.0
        for x in range(CB):
            block = block + jnp.where(
                ((lane & 63) >> 3) == x, turned(field[:, x], CB * (x - ky)), 0.0
            )
        for kx in range(2):
            blocks[kx * (CYC // CB) + ky] = block[kx]

    def chosen(t):
        number = kept[t]
        block = jnp.zeros((GROUPS, 8, LANES), F32)
        for k in range(BLOCKS):
            block = jnp.where(number == float(k), blocks[k], block)
        return block

    for t in other_tiles:
        block_out[t] = chosen(t)
        to_tile(block_out.at[t], block_in.at[tile], block_sem, t, tile).start()
    sent.append(
        lambda i: to_tile(
            block_out.at[tile_at(i)], block_in.at[tile], block_sem, tile_at(i), tile
        )
    )
    block_in[tile] = chosen(tile)

    load_weights.wait()

    def split_weights(f, carry):
        high, low = halves(weights[f])
        split[f, 0:64] = high
        split[f, 64:128] = low
        return carry

    lax.fori_loop(0, FINE, split_weights, 0)
    load_perturb.wait()
    pl.semaphore_wait(news.at[1], 3)
    tell(2, [mem_by(0, 1)])

    def wait_blocks(i, carry):
        t = tile_at(i)
        to_tile(block_out.at[t], block_in.at[t], block_sem, t, t).wait_recv()
        return carry

    lax.fori_loop(1, TILES, wait_blocks, 0)

    for f in range(FINE):
        value = block_in[block_list[0, f] >> 3]
        value = jnp.where(select[f] >= 0, value, turned(value, 64))
        high, low = halves(value.reshape(ROWS, LANES))
        product = jnp.dot(
            jnp.concatenate([high, low], axis=0), split[f], preferred_element_type=F32
        )
        product = product[:ROWS] + product[ROWS:]
        fine_a[pl.ds(f, ROWS, stride=FINE), :] = product[:, :LANES]
        fine_b[pl.ds(f, ROWS, stride=FINE), :] = product[:, LANES:]

    def share(i, carry):
        level = i
        for half, fine in enumerate((fine_a, fine_b)):
            sums = [jnp.zeros((FINE, LANES), F32)] * VARS
            for m in range(ROWS // LEV):
                row = m * LEV + level
                value = fine[pl.ds(pl.multiple_of(row * FINE, FINE), FINE), :]
                for v in range(VARS):
                    part = perturb[row * VARS + v, :, half * LANES : (half + 1) * LANES]
                    sums[v] = sums[v] + value * part.astype(F32)
            for v in range(VARS):
                slab[level * VARS + v, :, half * LANES : (half + 1) * LANES] = sums[v]
        return carry

    lax.fori_loop(0, LEV, share, 0)

    fine_of = (cells >> 8) == lax.broadcasted_iota(I32, (FINE, OBS), 0)
    high, low = halves(slab[...].reshape(SLABS * FINE, CELLS))
    at_cells = jnp.dot(
        jnp.concatenate([high, low], axis=1), cell_tall[...], preferred_element_type=F32
    )
    for s in range(SLABS):
        here = at_cells[s * FINE : (s + 1) * FINE]
        seen_out[s] = jnp.sum(jnp.where(fine_of, here, 0.0), axis=0, keepdims=True)
    pl.semaphore_wait(news.at[2], 1)
    for m in other_mems:
        to_member(seen_out.at[m], seen_in.at[mem], seen_sem, m, mem).start()
    sent.append(
        lambda i: to_member(
            seen_out.at[mem_at(i)], seen_in.at[mem], seen_sem, mem_at(i), mem
        )
    )
    seen_in[mem] = seen_out[mem]

    def wait_seen(i, carry):
        m = mem_at(i)
        to_member(seen_out.at[m], seen_in.at[m], seen_sem, m, m).wait_recv()
        return carry

    lax.fori_loop(1, N_MEM, wait_seen, 0)

    observed = jnp.sum(seen_in[...], axis=0)
    in_use = lane_of(1, OBS) < obs_count[0, 0]
    residual = jnp.where(in_use, obs_weight[...] * (observed - departures[...]), 0.0)
    weighted_out[...] = residual
    weighted[mem] = residual
    for m in other_mems:
        to_member(weighted.at[mem], weighted.at[mem], weighted_sem, m, mem).start()
    sent.append(
        lambda i: to_member(
            weighted.at[mem], weighted.at[mem], weighted_sem, mem_at(i), mem
        )
    )

    for m in other_mems:
        to_member(slab.at[m], slab_in.at[mem], slab_sem, m, mem).start()
    sent.append(
        lambda i: to_member(
            slab.at[mem_at(i)], slab_in.at[mem], slab_sem, mem_at(i), mem
        )
    )

    def wait_weighted(i, carry):
        m = mem_at(i)
        to_member(weighted.at[m], weighted.at[m], weighted_sem, m, m).wait_recv()
        return carry

    lax.fori_loop(1, N_MEM, wait_weighted, 0)

    for s in range(SLABS):
        high, low = halves(weighted[s])
        for i, part in enumerate((high, low)):
            spread[s * FINE : (s + 1) * FINE, i * OBS : (i + 1) * OBS] = jnp.where(
                fine_of, part.astype(F32), 0.0
            ).astype(BF16)
    forced = lax.dot_general(
        spread[...],
        cell_wide[...],
        (((1,), (1,)), ((), ())),
        preferred_element_type=F32,
    )
    forcing[...] = forced.reshape(SLABS, FINE, CELLS)

    def fine_gradient(level, carry):
        for half, fine in enumerate((fine_a, fine_b)):
            cut = slice(half * LANES, (half + 1) * LANES)
            parts = [forcing[level * VARS + v, :, cut] for v in range(VARS)]
            for m in range(ROWS // LEV):
                row = m * LEV + level
                value = sum(
                    perturb[row * VARS + v, :, cut].astype(F32) * parts[v]
                    for v in range(VARS)
                )
                fine[pl.ds(pl.multiple_of(row * FINE, FINE), FINE), :] = value
        return carry

    lax.fori_loop(0, LEV, fine_gradient, 0)

    for f in range(FINE):
        value = jnp.concatenate(
            [
                fine_a[pl.ds(f, ROWS, stride=FINE), :],
                fine_b[pl.ds(f, ROWS, stride=FINE), :],
            ],
            axis=1,
        )
        high, low = halves(value)
        product = lax.dot_general(
            jnp.concatenate([high, low], axis=0),
            split[f],
            (((1,), (1,)), ((), ())),
            preferred_element_type=F32,
        )
        product = product[:ROWS] + product[ROWS:]
        product = product + turned(product, 64)
        contrib[f] = product.reshape(GROUPS, 8, LANES)

    def returned(t):
        block = jnp.zeros((GROUPS, 8, LANES), F32)
        for f in range(FINE):
            block = block + jnp.where(select[f] == t, contrib[f], 0.0)
        return block

    for t in other_tiles:
        back_out[t] = returned(t)
        to_tile(back_out.at[t], back_in.at[tile], back_sem, t, tile).start()
    sent.append(
        lambda i: to_tile(
            back_out.at[tile_at(i)], back_in.at[tile], back_sem, tile_at(i), tile
        )
    )
    back_in[tile] = returned(tile)

    def wait_back(i, carry):
        t = tile_at(i)
        to_tile(back_out.at[t], back_in.at[t], back_sem, t, t).wait_recv()
        return carry

    lax.fori_loop(1, TILES, wait_back, 0)

    for k in range(BLOCKS):
        block = jnp.zeros((GROUPS, 8, LANES), F32)
        for t in range(TILES):
            block = block + jnp.where(kept[t] == float(k), back_in[t], 0.0)
        blocks[k] = block + turned(block, 64)

    coarse = []
    for x in range(CXC):
        plane = 0.0
        for ky in range(CYC // CB):
            plane = plane + jnp.where(
                (lane >> 3) == ky,
                turned(blocks[x // CB * (CYC // CB) + ky], CB * (ky - x % CB)),
                0.0,
            )
        coarse.append(plane)
    for i, message in enumerate(packed_halo(coarse, ty)):
        edge_out[i] = message
    second_halo = halo_copies(edge_out, edge_in, edge_sem)
    for copy in second_halo:
        copy.start()
    for copy in second_halo:
        copy.wait_recv()
    field = with_halo(coarse, edge_in, tx, ty)
    rate = rates[...][:, None]
    for sweep in range(SWEEPS):
        scaled = rate[sweep : 24 - sweep] * field
        inner = scaled[1:-1]
        beside = scaled[2:] + scaled[:-2] + turned(inner, 1) + turned(inner, -1)
        field = field[1:-1] + beside - 4.0 * inner
    field = field + planes[...]
    for x in range(CXC):
        rows[pl.ds(x, ROWS, stride=CXC), :] = field[x].reshape(ROWS, LANES)
    gradient[...] = rows[:, 0:CYC]

    def gather_slab(i, total):
        m = mem_at(i)
        to_member(slab.at[m], slab_in.at[m], slab_sem, m, m).wait_recv()
        return total + slab_in[m]

    increment[...] = lax.fori_loop(1, N_MEM, gather_slab, slab[mem])

    for copy in first_halo + second_halo:
        copy.wait_send()

    def wait_sent(i, carry):
        for of_peer in sent:
            of_peer(i).wait_send()
        return carry

    lax.fori_loop(1, TILES, wait_sent, 0)


def on_device(
    alpha,
    filter_rate,
    block_list,
    interp_weights,
    perturbations,
    obs_cells,
    obs_count,
    departures,
    obs_weight,
):
    in_vmem = pl.BlockSpec(memory_space=pltpu.VMEM)
    in_hbm = pl.BlockSpec(memory_space=pltpu.HBM)
    dma = pltpu.SemaphoreType.DMA
    increment, weighted, gradient = pl.pallas_call(
        kernel,
        out_shape=(
            jax.ShapeDtypeStruct((FINE, CELLS), F32),
            jax.ShapeDtypeStruct((1, OBS), F32),
            jax.ShapeDtypeStruct((ROWS * CXC, CYC), F32),
        ),
        in_specs=[in_hbm] * 9,
        out_specs=(in_vmem,) * 3,
        scratch_shapes=[
            pltpu.SMEM((1, FINE), I32),
            pltpu.SMEM((1, 1), I32),
            pltpu.VMEM((ROWS * CXC, CYC), F32),
            pltpu.VMEM((CXC, CYC), F32),
            pltpu.VMEM((1, OBS), I32),
            pltpu.VMEM((1, OBS), F32),
            pltpu.VMEM((1, OBS), F32),
            pltpu.VMEM((FINE, 64, CELLS), F32),
            pltpu.VMEM((ROWS * VARS, FINE, CELLS), BF16),
            pltpu.VMEM((FINE, 128, CELLS), BF16),
            pltpu.VMEM((ROWS * CXC, LANES), F32),
            pltpu.VMEM((CXC, GROUPS, 8, LANES), F32),
            pltpu.VMEM((CXC + 2 * SWEEPS, 8, LANES), F32),
            pltpu.VMEM((FINE, 8, LANES), I32),
            pltpu.VMEM((3, GROUPS + 1, 8, LANES), F32),
            pltpu.VMEM((5, GROUPS + 1, 8, LANES), F32),
            pltpu.VMEM((8, LANES), F32),
            pltpu.VMEM((TILES, 8, LANES), F32),
            pltpu.VMEM((TILES, 8, LANES), F32),
            pltpu.VMEM((BLOCKS, GROUPS, 8, LANES), F32),
            pltpu.VMEM((TILES, GROUPS, 8, LANES), F32),
            pltpu.VMEM((TILES, GROUPS, 8, LANES), F32),
            pltpu.VMEM((ROWS * FINE, LANES), F32),
            pltpu.VMEM((ROWS * FINE, LANES), F32),
            pltpu.VMEM((SLABS, FINE, CELLS), F32),
            pltpu.VMEM((SLABS, FINE, CELLS), F32),
            pltpu.VMEM((SLABS, 1, OBS), F32),
            pltpu.VMEM((SLABS, 1, OBS), F32),
            pltpu.VMEM((N_MEM, 1, OBS), F32),
            pltpu.VMEM((2 * CELLS, OBS), BF16),
            pltpu.VMEM((CELLS, 2 * OBS), BF16),
            pltpu.VMEM((SLABS * FINE, 2 * OBS), BF16),
            pltpu.VMEM((SLABS, FINE, CELLS), F32),
            pltpu.VMEM((FINE, GROUPS, 8, LANES), F32),
            pltpu.VMEM((TILES, GROUPS, 8, LANES), F32),
            pltpu.VMEM((TILES, GROUPS, 8, LANES), F32),
            pltpu.VMEM((3, GROUPS, 8, LANES), F32),
            pltpu.VMEM((5, GROUPS, 8, LANES), F32),
            dma((9,)),
            dma((2, 5)),
            dma((2, TILES)),
            dma((2, TILES)),
            dma((2, N_MEM)),
            dma((2, N_MEM)),
            dma((2, N_MEM)),
            dma((2, TILES)),
            dma((2, 5)),
            pltpu.SemaphoreType.REGULAR((3,)),
        ],
        compiler_params=pltpu.CompilerParams(
            collective_id=0, has_side_effects=True, vmem_limit_bytes=64 << 20
        ),
    )(
        block_list.reshape(1, FINE),
        obs_count.reshape(1, 1),
        alpha.reshape(ROWS * CXC, CYC),
        filter_rate,
        obs_cells.reshape(1, OBS),
        departures.reshape(1, OBS),
        obs_weight.reshape(1, OBS),
        interp_weights.reshape(FINE, 64, CELLS),
        perturbations.reshape(ROWS * VARS, FINE, CELLS),
    )
    return (
        increment.reshape(1, FINE, CELLS),
        weighted.reshape(departures.shape),
        gradient.reshape(alpha.shape),
    )


def solution(mesh):
    return jax.shard_map(
        on_device,
        mesh=mesh,
        in_specs=(
            P("mem", None, "tx", "ty"),
            P("tx", "ty"),
            P("tx", "ty", None),
            P("tx", "ty", None, None, None),
            P("mem", None, None, ("tx", "ty"), None),
            P("tx", "ty", None),
            P("tx", "ty"),
            P("tx", "ty", "mem", None),
            P("tx", "ty", "mem", None),
        ),
        out_specs=(
            P("mem", ("tx", "ty"), None),
            P("tx", "ty", "mem", None),
            P("mem", None, "tx", "ty"),
        ),
        check_vma=False,
    )
```

```python
import jax
import jax.numpy as jnp
from jax import lax
from jax.experimental import pallas as pl
from jax.experimental.pallas import tpu as pltpu
from jax.sharding import PartitionSpec as P

MESH = pl.DeviceIdType.MESH
F32, BF16, I32 = jnp.float32, jnp.bfloat16, jnp.int32

LEV = 4
VARS = 4
CB = 8
CXC = 16
CYC = 32
SWEEPS = 4
OBS = 512
ROWS = 32
GROUPS = ROWS // 8
FINE = 32
CELLS = 256
SLABS = 16
TILES = 16
N_MEM = 16
N_TX = 8
BLOCKS = 8
LANES = 128


def lane_of(*shape):
    return lax.broadcasted_iota(I32, shape, len(shape) - 1)


def turned(value, shift):
    if isinstance(shift, int):
        shift %= LANES
        if shift == 0:
            return value
    return pltpu.roll(value, shift, axis=value.ndim - 1)


def halves(value):
    high = value.astype(BF16)
    return high, (value - high.astype(F32)).astype(BF16)


def device_halo(tx, ty):
    below, above = lax.rem(tx + N_TX - 1, N_TX), lax.rem(tx + 1, N_TX)
    return ((below, ty), (above, ty), (below, 1 - ty), (above, 1 - ty), (tx, 1 - ty))


def packed_halo(planes, ty):
    lane = lane_of(8, LANES)
    first = sum(turned(planes[j], CYC * j) for j in range(SWEEPS))
    last = sum(turned(planes[CXC - SWEEPS + j], CYC * j) for j in range(SWEEPS))
    start = (CYC - SWEEPS) * (1 - ty)
    side = 0.0
    for x in range(CXC):
        shift = lax.rem(SWEEPS * x - start + LANES, LANES)
        side = side + jnp.where(lane >> 2 == x, turned(planes[x], shift), 0.0)
    return first, last, side


def with_halo(planes, halo, tx, ty):
    lane = lane_of(8, LANES)
    own = lane < CYC
    side = (lane >> 2) == jnp.where(ty == 0, CYC // 4, LANES // 4 - 1)
    corner = jnp.where(ty == 0, CYC, 3 * CYC)
    place = jnp.where(ty == 0, CYC, LANES - SWEEPS)

    def beyond(straight, across, there):
        made = []
        for j in range(SWEEPS):
            plane = jnp.where(own, turned(straight, -CYC * j), 0.0)
            shift = lax.rem(corner - CYC * j + LANES, LANES)
            plane = plane + jnp.where(side, turned(across, shift), 0.0)
            made.append(jnp.where(there, plane, 0.0))
        return made

    low = beyond(halo[1], halo[3], tx > 0)
    high = beyond(halo[0], halo[2], tx < N_TX - 1)
    middle = []
    for x in range(CXC):
        shift = lax.rem(place - SWEEPS * x + LANES, LANES)
        middle.append(planes[x] + jnp.where(side, turned(halo[4], shift), 0.0))
    return jnp.stack(low + middle + high)


def kernel(
    block_list_hbm,
    obs_count_hbm,
    alpha_hbm,
    filter_rate_hbm,
    obs_cells_hbm,
    departures_hbm,
    obs_weight_hbm,
    weights_hbm,
    perturb_hbm,
    increment_hbm,
    weighted_hbm,
    gradient_hbm,
    increment,
    gradient,
    block_list,
    obs_count,
    alpha,
    filter_rate,
    obs_cells,
    departures,
    obs_weight,
    weights,
    perturb,
    split,
    rows,
    planes,
    rates,
    select,
    halo_out,
    halo_in,
    code_out,
    code_in,
    kept,
    blocks,
    block_out,
    block_in,
    fine_a,
    fine_b,
    slab,
    slab_in,
    weighted,
    seen_out,
    seen_in,
    cell_tall,
    cell_wide,
    spread,
    forcing,
    contrib,
    back_out,
    back_in,
    edge_out,
    edge_in,
    load_sem,
    halo_sem,
    code_sem,
    block_sem,
    slab_sem,
    weighted_sem,
    seen_sem,
    back_sem,
    edge_sem,
    news,
    store_sem,
):
    mem, tx, ty = lax.axis_index("mem"), lax.axis_index("tx"), lax.axis_index("ty")
    tile = tx * 2 + ty
    lane = lane_of(8, LANES)
    sent = []

    loads = [
        pltpu.make_async_copy(source, target, load_sem.at[i])
        for i, (source, target) in enumerate(
            (
                (alpha_hbm, alpha),
                (filter_rate_hbm, filter_rate),
                (block_list_hbm, block_list),
                (obs_count_hbm, obs_count),
                (obs_cells_hbm, obs_cells),
                (departures_hbm, departures),
                (obs_weight_hbm, obs_weight),
                (weights_hbm, weights),
                (perturb_hbm, perturb),
            )
        )
    ]
    for load in loads:
        load.start()
    load_weights, load_perturb = loads[7:]
    stores = [
        pltpu.make_async_copy(source, target, store_sem.at[i])
        for i, (source, target) in enumerate(
            (
                (increment, increment_hbm),
                (weighted.at[lax.axis_index("mem")], weighted_hbm),
                (gradient, gradient_hbm),
            )
        )
    ]

    y, core = lax.div(tx, 2), lax.rem(tx, 2)
    z, run = lax.div(mem, 2), lax.rem(mem, 2)

    def tile_by(dy, dcore, dty):
        to_core = 1 - core if dcore else core
        return (lax.rem(y + dy, 4) * 2 + to_core) * 2 + (1 - ty if dty else ty)

    def mem_by(dz, drun):
        return lax.rem(z + dz, 8) * 2 + (1 - run if drun else run)

    other_tiles = [
        tile_by(dy, dcore, dty) for dty in (1, 0) for dy in (2, 1, 3, 0) for dcore in (1, 0)
    ][:-1]
    other_mems = [
        mem_by(dz, drun) for dz in (4, 3, 5, 2, 6, 1, 7, 0) for drun in (1, 0)
    ][:-1]

    def tile_at(i):
        return lax.rem(tile + i, TILES)

    def tile_device(t):
        return {"tx": lax.div(t, 2), "ty": lax.rem(t, 2)}

    def mem_at(i):
        return lax.rem(mem + i, N_MEM)

    beside_mems = [mem_by(1, 0), mem_by(7, 0), mem_by(0, 1)]
    two_off_mems = [mem_by(2, 0), mem_by(6, 0), mem_by(0, 1)]
    barrier = pltpu.get_barrier_semaphore()
    for t in other_tiles:
        pl.semaphore_signal(
            barrier, inc=1, device_id=tile_device(t), device_id_type=MESH
        )
    for m in beside_mems:
        pl.semaphore_signal(barrier, inc=1, device_id={"mem": m}, device_id_type=MESH)

    def tell(step, members):
        for m in members:
            pl.semaphore_signal(
                news.at[step], inc=1, device_id={"mem": m}, device_id_type=MESH
            )

    def to_tile(src, dst, sem, t, slot):
        return pltpu.make_async_remote_copy(
            src_ref=src,
            dst_ref=dst,
            send_sem=sem.at[0, t],
            recv_sem=sem.at[1, slot],
            device_id=tile_device(t),
            device_id_type=MESH,
        )

    def to_member(src, dst, sem, m, slot):
        return pltpu.make_async_remote_copy(
            src_ref=src,
            dst_ref=dst,
            send_sem=sem.at[0, m],
            recv_sem=sem.at[1, slot],
            device_id={"mem": m},
            device_id_type=MESH,
        )

    def halo_copies(out, into, sem):
        sources = (0, 1, 0, 1, 2)
        return [
            pltpu.make_async_remote_copy(
                src_ref=out.at[sources[i]],
                dst_ref=into.at[i],
                send_sem=sem.at[0, i],
                recv_sem=sem.at[1, i],
                device_id={"tx": x, "ty": y},
                device_id_type=MESH,
            )
            for i, (x, y) in enumerate(device_halo(tx, ty))
        ]

    rows[...] = jnp.zeros_like(rows)
    rates[...] = jnp.zeros_like(rates)
    for load in loads[:7]:
        load.wait()
    rows[:, 0:CYC] = alpha[...]
    for x in range(CXC):
        planes[x] = rows[pl.ds(x, ROWS, stride=CXC), :].reshape(GROUPS, 8, LANES)
        rates[SWEEPS + x, :, 0:CYC] = jnp.broadcast_to(
            filter_rate[x : x + 1, :], (8, CYC)
        )
    both = jnp.concatenate(
        [planes[...], rates[SWEEPS : SWEEPS + CXC][:, None]], axis=1
    )
    for i, message in enumerate(packed_halo(both, ty)):
        halo_out[i] = message

    asked = lane < 0
    for f in range(FINE):
        asked = asked | (lane == block_list[0, f])
    asked = jnp.where(asked, 1.0, 0.0)
    second = jnp.zeros((8, LANES), F32)
    for j in range(1, BLOCKS):
        second = jnp.maximum(second, jnp.where((lane & 7) >= j, turned(asked, j), 0.0))
    code_out[...] = asked * (1.0 + second)

    pl.semaphore_wait(barrier, TILES - 1 + 3)
    first_halo = halo_copies(halo_out, halo_in, halo_sem)
    for t in other_tiles[:6]:
        to_tile(code_out, code_in.at[tile], code_sem, t, tile).start()
    for copy in first_halo:
        copy.start()
    for t in other_tiles[6:]:
        to_tile(code_out, code_in.at[tile], code_sem, t, tile).start()
    tell(0, beside_mems)
    sent.append(lambda i: to_tile(code_out, code_in.at[tile], code_sem, tile_at(i), tile))
    code_in[tile] = code_out[...]

    side_half = jnp.where(lane < 64, 0.0, 1.0)
    for f in range(FINE):
        wanted = block_list[0, f]
        rank = jnp.max(jnp.where(lane == wanted, second, 0.0), axis=1, keepdims=True)
        select[f] = jnp.where(side_half == rank, wanted >> 3, -1)

    cells = obs_cells[...]
    cell_hot = jnp.where(
        lax.broadcasted_iota(I32, (CELLS, OBS), 0) == (cells & (CELLS - 1)), 1.0, 0.0
    ).astype(BF16)
    for i in range(2):
        cell_tall[i * CELLS : (i + 1) * CELLS, :] = cell_hot
        cell_wide[:, i * OBS : (i + 1) * OBS] = cell_hot

    def wait_code(i, carry):
        t = tile_at(i)
        to_tile(code_out, code_in.at[t], code_sem, t, t).wait_recv()
        return carry

    lax.fori_loop(1, TILES, wait_code, 0)
    lane3 = lane_of(TILES, 8, LANES)
    mine = (lane3 >> 3) == tile
    local = (lane3 & 7).astype(F32)
    codes = code_in[...]
    slot_0 = jnp.sum(jnp.where(mine & (codes == 1.0), local, 0.0), axis=2, keepdims=True)
    slot_1 = jnp.sum(jnp.where(mine & (codes == 2.0), local, 0.0), axis=2, keepdims=True)
    kept[...] = jnp.where(lane3 < 64, slot_0, slot_1)

    for copy in first_halo:
        copy.wait_recv()
    pl.semaphore_wait(news.at[0], 3)
    tell(1, two_off_mems)

    whole = with_halo(both, halo_in, tx, ty)
    field, rate = whole[:, :GROUPS], whole[:, GROUPS:]
    rates[...] = rate[:, 0]
    for sweep in range(SWEEPS):
        center = field[1:-1]
        beside = field[2:] + field[:-2] + turned(center, 1) + turned(center, -1)
        field = center + rate[1 + sweep : 23 - sweep] * (beside - 4.0 * center)

    field = jnp.where(lane < CYC, field, 0.0)
    field = (field + turned(field, 64)).reshape(2, CB, GROUPS, 8, LANES)
    for ky in range(CYC // CB):
        block = 0.0
        for x in range(CB):
            block = block + jnp.where(
                ((lane & 63) >> 3) == x, turned(field[:, x], CB * (x - ky)), 0.0
            )
        for kx in range(2):
            blocks[kx * (CYC // CB) + ky] = block[kx]

    def chosen(t):
        number = kept[t]
        block = jnp.zeros((GROUPS, 8, LANES), F32)
        for k in range(BLOCKS):
            block = jnp.where(number == float(k), blocks[k], block)
        return block

    for t in other_tiles:
        block_out[t] = chosen(t)
        to_tile(block_out.at[t], block_in.at[tile], block_sem, t, tile).start()
    sent.append(
        lambda i: to_tile(
            block_out.at[tile_at(i)], block_in.at[tile], block_sem, tile_at(i), tile
        )
    )
    block_in[tile] = chosen(tile)

    load_weights.wait()

    def split_weights(f, carry):
        high, low = halves(weights[f])
        split[f, 0:64] = high
        split[f, 64:128] = low
        return carry

    lax.fori_loop(0, FINE, split_weights, 0)
    load_perturb.wait()
    pl.semaphore_wait(news.at[1], 3)
    tell(2, [mem_by(0, 1)])

    def wait_blocks(i, carry):
        t = tile_at(i)
        to_tile(block_out.at[t], block_in.at[t], block_sem, t, t).wait_recv()
        return carry

    lax.fori_loop(1, TILES, wait_blocks, 0)

    for f in range(FINE):
        value = block_in[block_list[0, f] >> 3]
        value = jnp.where(select[f] >= 0, value, turned(value, 64))
        high, low = halves(value.reshape(ROWS, LANES))
        product = jnp.dot(
            jnp.concatenate([high, low], axis=0), split[f], preferred_element_type=F32
        )
        product = product[:ROWS] + product[ROWS:]
        fine_a[pl.ds(f, ROWS, stride=FINE), :] = product[:, :LANES]
        fine_b[pl.ds(f, ROWS, stride=FINE), :] = product[:, LANES:]

    def share(i, carry):
        level = i
        for half, fine in enumerate((fine_a, fine_b)):
            sums = [jnp.zeros((FINE, LANES), F32)] * VARS
            for m in range(ROWS // LEV):
                row = m * LEV + level
                value = fine[pl.ds(pl.multiple_of(row * FINE, FINE), FINE), :]
                for v in range(VARS):
                    part = perturb[row * VARS + v, :, half * LANES : (half + 1) * LANES]
                    sums[v] = sums[v] + value * part.astype(F32)
            for v in range(VARS):
                slab[level * VARS + v, :, half * LANES : (half + 1) * LANES] = sums[v]
        return carry

    lax.fori_loop(0, LEV, share, 0)

    fine_of = (cells >> 8) == lax.broadcasted_iota(I32, (FINE, OBS), 0)
    high, low = halves(slab[...].reshape(SLABS * FINE, CELLS))
    at_cells = jnp.dot(
        jnp.concatenate([high, low], axis=1), cell_tall[...], preferred_element_type=F32
    )
    for s in range(SLABS):
        here = at_cells[s * FINE : (s + 1) * FINE]
        seen_out[s] = jnp.sum(jnp.where(fine_of, here, 0.0), axis=0, keepdims=True)
    pl.semaphore_wait(news.at[2], 1)
    for m in other_mems:
        to_member(seen_out.at[m], seen_in.at[mem], seen_sem, m, mem).start()
    sent.append(
        lambda i: to_member(
            seen_out.at[mem_at(i)], seen_in.at[mem], seen_sem, mem_at(i), mem
        )
    )
    seen_in[mem] = seen_out[mem]

    def wait_seen(i, carry):
        m = mem_at(i)
        to_member(seen_out.at[m], seen_in.at[m], seen_sem, m, m).wait_recv()
        return carry

    lax.fori_loop(1, N_MEM, wait_seen, 0)

    observed = jnp.sum(seen_in[...], axis=0)
    in_use = lane_of(1, OBS) < obs_count[0, 0]
    residual = jnp.where(in_use, obs_weight[...] * (observed - departures[...]), 0.0)
    weighted[mem] = residual
    for m in other_mems:
        to_member(weighted.at[mem], weighted.at[mem], weighted_sem, m, mem).start()
    sent.append(
        lambda i: to_member(
            weighted.at[mem], weighted.at[mem], weighted_sem, mem_at(i), mem
        )
    )

    stores[1].start()

    def wait_weighted(i, carry):
        m = mem_at(i)
        to_member(weighted.at[m], weighted.at[m], weighted_sem, m, m).wait_recv()
        return carry

    lax.fori_loop(1, N_MEM, wait_weighted, 0)

    for m in other_mems:
        to_member(slab.at[m], slab_in.at[mem], slab_sem, m, mem).start()
    sent.append(
        lambda i: to_member(
            slab.at[mem_at(i)], slab_in.at[mem], slab_sem, mem_at(i), mem
        )
    )

    for s in range(SLABS):
        high, low = halves(weighted[s])
        for i, part in enumerate((high, low)):
            spread[s * FINE : (s + 1) * FINE, i * OBS : (i + 1) * OBS] = jnp.where(
                fine_of, part.astype(F32), 0.0
            ).astype(BF16)
    forced = lax.dot_general(
        spread[...],
        cell_wide[...],
        (((1,), (1,)), ((), ())),
        preferred_element_type=F32,
    )
    forcing[...] = forced.reshape(SLABS, FINE, CELLS)

    def fine_gradient(level, carry):
        for half, fine in enumerate((fine_a, fine_b)):
            cut = slice(half * LANES, (half + 1) * LANES)
            parts = [forcing[level * VARS + v, :, cut] for v in range(VARS)]
            for m in range(ROWS // LEV):
                row = m * LEV + level
                value = sum(
                    perturb[row * VARS + v, :, cut].astype(F32) * parts[v]
                    for v in range(VARS)
                )
                fine[pl.ds(pl.multiple_of(row * FINE, FINE), FINE), :] = value
        return carry

    lax.fori_loop(0, LEV, fine_gradient, 0)

    for f in range(FINE):
        value = jnp.concatenate(
            [
                fine_a[pl.ds(f, ROWS, stride=FINE), :],
                fine_b[pl.ds(f, ROWS, stride=FINE), :],
            ],
            axis=1,
        )
        high, low = halves(value)
        product = lax.dot_general(
            jnp.concatenate([high, low], axis=0),
            split[f],
            (((1,), (1,)), ((), ())),
            preferred_element_type=F32,
        )
        product = product[:ROWS] + product[ROWS:]
        product = product + turned(product, 64)
        contrib[f] = product.reshape(GROUPS, 8, LANES)

    def returned(t):
        block = jnp.zeros((GROUPS, 8, LANES), F32)
        for f in range(FINE):
            block = block + jnp.where(select[f] == t, contrib[f], 0.0)
        return block

    for t in other_tiles:
        back_out[t] = returned(t)
        to_tile(back_out.at[t], back_in.at[tile], back_sem, t, tile).start()
    sent.append(
        lambda i: to_tile(
            back_out.at[tile_at(i)], back_in.at[tile], back_sem, tile_at(i), tile
        )
    )
    back_in[tile] = returned(tile)

    def wait_back(i, carry):
        t = tile_at(i)
        to_tile(back_out.at[t], back_in.at[t], back_sem, t, t).wait_recv()
        return carry

    lax.fori_loop(1, TILES, wait_back, 0)

    for k in range(BLOCKS):
        block = jnp.zeros((GROUPS, 8, LANES), F32)
        for t in range(TILES):
            block = block + jnp.where(kept[t] == float(k), back_in[t], 0.0)
        blocks[k] = block + turned(block, 64)

    coarse = []
    for x in range(CXC):
        plane = 0.0
        for ky in range(CYC // CB):
            plane = plane + jnp.where(
                (lane >> 3) == ky,
                turned(blocks[x // CB * (CYC // CB) + ky], CB * (ky - x % CB)),
                0.0,
            )
        coarse.append(plane)
    for i, message in enumerate(packed_halo(coarse, ty)):
        edge_out[i] = message
    second_halo = halo_copies(edge_out, edge_in, edge_sem)
    for copy in second_halo:
        copy.start()
    for copy in second_halo:
        copy.wait_recv()
    field = with_halo(coarse, edge_in, tx, ty)
    rate = rates[...][:, None]
    for sweep in range(SWEEPS):
        scaled = rate[sweep : 24 - sweep] * field
        inner = scaled[1:-1]
        beside = scaled[2:] + scaled[:-2] + turned(inner, 1) + turned(inner, -1)
        field = field[1:-1] + beside - 4.0 * inner
    field = field + planes[...]
    for x in range(CXC):
        rows[pl.ds(x, ROWS, stride=CXC), :] = field[x].reshape(ROWS, LANES)
    gradient[...] = rows[:, 0:CYC]
    stores[2].start()

    def gather_slab(i, total):
        m = mem_at(i)
        to_member(slab.at[m], slab_in.at[m], slab_sem, m, m).wait_recv()
        return total + slab_in[m]

    increment[...] = lax.fori_loop(1, N_MEM, gather_slab, slab[mem])
    stores[0].start()

    for copy in first_halo + second_halo:
        copy.wait_send()

    def wait_sent(i, carry):
        for of_peer in sent:
            of_peer(i).wait_send()
        return carry

    lax.fori_loop(1, TILES, wait_sent, 0)
    for store in stores:
        store.wait()


def handed_on(*refs):
    sources, targets, held, load_sem, store_sem = (
        refs[:3],
        refs[3:6],
        refs[6:9],
        refs[9],
        refs[10],
    )
    loads = [
        pltpu.make_async_copy(source, here, load_sem.at[i])
        for i, (source, here) in enumerate(zip(sources, held))
    ]
    stores = [
        pltpu.make_async_copy(here, target, store_sem.at[i])
        for i, (here, target) in enumerate(zip(held, targets))
    ]
    for load in loads:
        load.start()
    for load, store in zip(loads, stores):
        load.wait()
        store.start()
    for store in stores:
        store.wait()


def on_device(
    alpha,
    filter_rate,
    block_list,
    interp_weights,
    perturbations,
    obs_cells,
    obs_count,
    departures,
    obs_weight,
):
    in_hbm = pl.BlockSpec(memory_space=pltpu.HBM)
    dma = pltpu.SemaphoreType.DMA
    results = (
        jax.ShapeDtypeStruct((FINE, CELLS), F32),
        jax.ShapeDtypeStruct((1, OBS), F32),
        jax.ShapeDtypeStruct((ROWS * CXC, CYC), F32),
    )
    made = pl.pallas_call(
        kernel,
        out_shape=results,
        in_specs=[in_hbm] * 9,
        out_specs=(in_hbm,) * 3,
        scratch_shapes=[
            pltpu.VMEM((FINE, CELLS), F32),
            pltpu.VMEM((ROWS * CXC, CYC), F32),
            pltpu.SMEM((1, FINE), I32),
            pltpu.SMEM((1, 1), I32),
            pltpu.VMEM((ROWS * CXC, CYC), F32),
            pltpu.VMEM((CXC, CYC), F32),
            pltpu.VMEM((1, OBS), I32),
            pltpu.VMEM((1, OBS), F32),
            pltpu.VMEM((1, OBS), F32),
            pltpu.VMEM((FINE, 64, CELLS), F32),
            pltpu.VMEM((ROWS * VARS, FINE, CELLS), BF16),
            pltpu.VMEM((FINE, 128, CELLS), BF16),
            pltpu.VMEM((ROWS * CXC, LANES), F32),
            pltpu.VMEM((CXC, GROUPS, 8, LANES), F32),
            pltpu.VMEM((CXC + 2 * SWEEPS, 8, LANES), F32),
            pltpu.VMEM((FINE, 8, LANES), I32),
            pltpu.VMEM((3, GROUPS + 1, 8, LANES), F32),
            pltpu.VMEM((5, GROUPS + 1, 8, LANES), F32),
            pltpu.VMEM((8, LANES), F32),
            pltpu.VMEM((TILES, 8, LANES), F32),
            pltpu.VMEM((TILES, 8, LANES), F32),
            pltpu.VMEM((BLOCKS, GROUPS, 8, LANES), F32),
            pltpu.VMEM((TILES, GROUPS, 8, LANES), F32),
            pltpu.VMEM((TILES, GROUPS, 8, LANES), F32),
            pltpu.VMEM((ROWS * FINE, LANES), F32),
            pltpu.VMEM((ROWS * FINE, LANES), F32),
            pltpu.VMEM((SLABS, FINE, CELLS), F32),
            pltpu.VMEM((SLABS, FINE, CELLS), F32),
            pltpu.VMEM((SLABS, 1, OBS), F32),
            pltpu.VMEM((SLABS, 1, OBS), F32),
            pltpu.VMEM((N_MEM, 1, OBS), F32),
            pltpu.VMEM((2 * CELLS, OBS), BF16),
            pltpu.VMEM((CELLS, 2 * OBS), BF16),
            pltpu.VMEM((SLABS * FINE, 2 * OBS), BF16),
            pltpu.VMEM((SLABS, FINE, CELLS), F32),
            pltpu.VMEM((FINE, GROUPS, 8, LANES), F32),
            pltpu.VMEM((TILES, GROUPS, 8, LANES), F32),
            pltpu.VMEM((TILES, GROUPS, 8, LANES), F32),
            pltpu.VMEM((3, GROUPS, 8, LANES), F32),
            pltpu.VMEM((5, GROUPS, 8, LANES), F32),
            dma((9,)),
            dma((2, 5)),
            dma((2, TILES)),
            dma((2, TILES)),
            dma((2, N_MEM)),
            dma((2, N_MEM)),
            dma((2, N_MEM)),
            dma((2, TILES)),
            dma((2, 5)),
            pltpu.SemaphoreType.REGULAR((3,)),
            dma((3,)),
        ],
        compiler_params=pltpu.CompilerParams(
            collective_id=0, has_side_effects=True, vmem_limit_bytes=64 << 20
        ),
    )(
        block_list.reshape(1, FINE),
        obs_count.reshape(1, 1),
        alpha.reshape(ROWS * CXC, CYC),
        filter_rate,
        obs_cells.reshape(1, OBS),
        departures.reshape(1, OBS),
        obs_weight.reshape(1, OBS),
        interp_weights.reshape(FINE, 64, CELLS),
        perturbations.reshape(ROWS * VARS, FINE, CELLS),
    )
    increment, weighted, gradient = pl.pallas_call(
        handed_on,
        out_shape=results,
        in_specs=[in_hbm] * 3,
        out_specs=(in_hbm,) * 3,
        scratch_shapes=[pltpu.VMEM(r.shape, r.dtype) for r in results]
        + [dma((3,)), dma((3,))],
        compiler_params=pltpu.CompilerParams(vmem_limit_bytes=64 << 20),
    )(*made)
    return (
        increment.reshape(1, FINE, CELLS),
        weighted.reshape(departures.shape),
        gradient.reshape(alpha.shape),
    )


def solution(mesh):
    return jax.shard_map(
        on_device,
        mesh=mesh,
        in_specs=(
            P("mem", None, "tx", "ty"),
            P("tx", "ty"),
            P("tx", "ty", None),
            P("tx", "ty", None, None, None),
            P("mem", None, None, ("tx", "ty"), None),
            P("tx", "ty", None),
            P("tx", "ty"),
            P("tx", "ty", "mem", None),
            P("tx", "ty", "mem", None),
        ),
        out_specs=(
            P("mem", ("tx", "ty"), None),
            P("tx", "ty", "mem", None),
            P("mem", None, "tx", "ty"),
        ),
        check_vma=False,
    )
```

```python
import jax
import jax.numpy as jnp
from jax import lax
from jax.experimental import pallas as pl
from jax.experimental.pallas import tpu as pltpu
from jax.sharding import PartitionSpec as P

MESH = pl.DeviceIdType.MESH
F32, BF16, I32 = jnp.float32, jnp.bfloat16, jnp.int32

LEV = 4
VARS = 4
CB = 8
CXC = 16
CYC = 32
SWEEPS = 4
OBS = 512
ROWS = 32
GROUPS = ROWS // 8
FINE = 32
CELLS = 256
SLABS = 16
QUARTER = 4
HALF = 8
TILES = 16
N_MEM = 16
N_TX = 8
BLOCKS = 8
LANES = 128


def lane_of(*shape):
    return lax.broadcasted_iota(I32, shape, len(shape) - 1)


def turned(value, shift):
    if isinstance(shift, int):
        shift %= LANES
        if shift == 0:
            return value
    return pltpu.roll(value, shift, axis=value.ndim - 1)


def halves(value):
    high = value.astype(BF16)
    return high, (value - high.astype(F32)).astype(BF16)


def device_halo(tx, ty):
    below, above = lax.rem(tx + N_TX - 1, N_TX), lax.rem(tx + 1, N_TX)
    return ((below, ty), (above, ty), (below, 1 - ty), (above, 1 - ty), (tx, 1 - ty))


def packed_halo(planes, ty):
    lane = lane_of(8, LANES)
    first = sum(turned(planes[j], CYC * j) for j in range(SWEEPS))
    last = sum(turned(planes[CXC - SWEEPS + j], CYC * j) for j in range(SWEEPS))
    start = (CYC - SWEEPS) * (1 - ty)
    side = 0.0
    for x in range(CXC):
        shift = lax.rem(SWEEPS * x - start + LANES, LANES)
        side = side + jnp.where(lane >> 2 == x, turned(planes[x], shift), 0.0)
    return first, last, side


def with_halo(planes, halo, tx, ty):
    lane = lane_of(8, LANES)
    own = lane < CYC
    side = (lane >> 2) == jnp.where(ty == 0, CYC // 4, LANES // 4 - 1)
    corner = jnp.where(ty == 0, CYC, 3 * CYC)
    place = jnp.where(ty == 0, CYC, LANES - SWEEPS)

    def beyond(straight, across, there):
        made = []
        for j in range(SWEEPS):
            plane = jnp.where(own, turned(straight, -CYC * j), 0.0)
            shift = lax.rem(corner - CYC * j + LANES, LANES)
            plane = plane + jnp.where(side, turned(across, shift), 0.0)
            made.append(jnp.where(there, plane, 0.0))
        return made

    low = beyond(halo[1], halo[3], tx > 0)
    high = beyond(halo[0], halo[2], tx < N_TX - 1)
    middle = []
    for x in range(CXC):
        shift = lax.rem(place - SWEEPS * x + LANES, LANES)
        middle.append(planes[x] + jnp.where(side, turned(halo[4], shift), 0.0))
    return jnp.stack(low + middle + high)


def kernel(
    block_list_hbm,
    obs_count_hbm,
    alpha_hbm,
    filter_rate_hbm,
    obs_cells_hbm,
    departures_hbm,
    obs_weight_hbm,
    weights_hbm,
    perturb_hbm,
    increment_hbm,
    weighted_hbm,
    gradient_hbm,
    increment,
    gradient,
    block_list,
    obs_count,
    alpha,
    filter_rate,
    obs_cells,
    departures,
    obs_weight,
    weights,
    perturb,
    split,
    rows,
    planes,
    rates,
    select,
    halo_out,
    halo_in,
    code_out,
    code_in,
    kept,
    blocks,
    block_out,
    block_in,
    fine_a,
    fine_b,
    slab,
    paired,
    paired_in,
    slab_in,
    weighted,
    seen_out,
    seen_in,
    observations,
    partial,
    cell_tall,
    cell_wide,
    spread,
    forcing,
    contrib,
    back_out,
    back_in,
    edge_out,
    edge_in,
    load_sem,
    halo_sem,
    code_sem,
    block_sem,
    pair_sem,
    slab_sem,
    observed_sem,
    seen_sem,
    partial_sem,
    back_sem,
    edge_sem,
    news,
    store_sem,
):
    mem, tx, ty = lax.axis_index("mem"), lax.axis_index("tx"), lax.axis_index("ty")
    tile = tx * 2 + ty
    lane = lane_of(8, LANES)
    sent = []

    loads = [
        pltpu.make_async_copy(source, target, load_sem.at[i])
        for i, (source, target) in enumerate(
            (
                (alpha_hbm, alpha),
                (filter_rate_hbm, filter_rate),
                (block_list_hbm, block_list),
                (obs_count_hbm, obs_count),
                (obs_cells_hbm, obs_cells),
                (departures_hbm, departures),
                (obs_weight_hbm, obs_weight),
                (weights_hbm, weights),
                (perturb_hbm, perturb),
            )
        )
    ]
    for load in loads:
        load.start()
    load_weights, load_perturb = loads[7:]
    stores = [
        pltpu.make_async_copy(source, target, store_sem.at[i])
        for i, (source, target) in enumerate(
            (
                (increment, increment_hbm),
                (weighted.at[lax.axis_index("mem")], weighted_hbm),
                (gradient, gradient_hbm),
            )
        )
    ]

    y, core = lax.div(tx, 2), lax.rem(tx, 2)
    z, run = lax.div(mem, 2), lax.rem(mem, 2)

    def tile_by(dy, dcore, dty):
        to_core = 1 - core if dcore else core
        return (lax.rem(y + dy, 4) * 2 + to_core) * 2 + (1 - ty if dty else ty)

    def mem_by(dz, drun):
        return lax.rem(z + dz, 8) * 2 + (1 - run if drun else run)

    other_tiles = [
        tile_by(dy, dcore, dty) for dty in (1, 0) for dy in (2, 1, 3, 0) for dcore in (1, 0)
    ][:-1]
    other_mems = [
        mem_by(dz, drun) for dz in (4, 3, 5, 2, 6, 1, 7, 0) for drun in (1, 0)
    ][:-1]

    def tile_at(i):
        return lax.rem(tile + i, TILES)

    def tile_device(t):
        return {"tx": lax.div(t, 2), "ty": lax.rem(t, 2)}

    def mem_at(i):
        return lax.rem(mem + i, N_MEM)

    beside_mems = [mem_by(1, 0), mem_by(7, 0), mem_by(0, 1)]
    two_off_mems = [mem_by(2, 0), mem_by(6, 0), mem_by(0, 1)]
    barrier = pltpu.get_barrier_semaphore()
    for t in other_tiles:
        pl.semaphore_signal(
            barrier, inc=1, device_id=tile_device(t), device_id_type=MESH
        )
    for m in beside_mems:
        pl.semaphore_signal(barrier, inc=1, device_id={"mem": m}, device_id_type=MESH)

    def tell(step, members):
        for m in members:
            pl.semaphore_signal(
                news.at[step], inc=1, device_id={"mem": m}, device_id_type=MESH
            )

    def to_tile(src, dst, sem, t, slot):
        return pltpu.make_async_remote_copy(
            src_ref=src,
            dst_ref=dst,
            send_sem=sem.at[0, t],
            recv_sem=sem.at[1, slot],
            device_id=tile_device(t),
            device_id_type=MESH,
        )

    def to_member(src, dst, sem, m, slot):
        return pltpu.make_async_remote_copy(
            src_ref=src,
            dst_ref=dst,
            send_sem=sem.at[0, m],
            recv_sem=sem.at[1, slot],
            device_id={"mem": m},
            device_id_type=MESH,
        )

    def to_member_quarter(src, dst, sem, m, theirs, mine):
        return pltpu.make_async_remote_copy(
            src_ref=src.at[theirs],
            dst_ref=dst.at[mine],
            send_sem=sem.at[0, theirs],
            recv_sem=sem.at[1, mine],
            device_id={"mem": m},
            device_id_type=MESH,
        )

    def halo_copies(out, into, sem):
        sources = (0, 1, 0, 1, 2)
        return [
            pltpu.make_async_remote_copy(
                src_ref=out.at[sources[i]],
                dst_ref=into.at[i],
                send_sem=sem.at[0, i],
                recv_sem=sem.at[1, i],
                device_id={"tx": x, "ty": y},
                device_id_type=MESH,
            )
            for i, (x, y) in enumerate(device_halo(tx, ty))
        ]

    rows[...] = jnp.zeros_like(rows)
    rates[...] = jnp.zeros_like(rates)
    for load in loads[:7]:
        load.wait()
    rows[:, 0:CYC] = alpha[...]
    for x in range(CXC):
        planes[x] = rows[pl.ds(x, ROWS, stride=CXC), :].reshape(GROUPS, 8, LANES)
        rates[SWEEPS + x, :, 0:CYC] = jnp.broadcast_to(
            filter_rate[x : x + 1, :], (8, CYC)
        )
    both = jnp.concatenate(
        [planes[...], rates[SWEEPS : SWEEPS + CXC][:, None]], axis=1
    )
    for i, message in enumerate(packed_halo(both, ty)):
        halo_out[i] = message

    asked = lane < 0
    for f in range(FINE):
        asked = asked | (lane == block_list[0, f])
    asked = jnp.where(asked, 1.0, 0.0)
    second = jnp.zeros((8, LANES), F32)
    for j in range(1, BLOCKS):
        second = jnp.maximum(second, jnp.where((lane & 7) >= j, turned(asked, j), 0.0))
    code_out[...] = asked * (1.0 + second)

    pl.semaphore_wait(barrier, TILES - 1 + 3)
    first_halo = halo_copies(halo_out, halo_in, halo_sem)
    for t in other_tiles[:6]:
        to_tile(code_out, code_in.at[tile], code_sem, t, tile).start()
    for copy in first_halo:
        copy.start()
    for t in other_tiles[6:]:
        to_tile(code_out, code_in.at[tile], code_sem, t, tile).start()
    tell(0, beside_mems)
    sent.append(lambda i: to_tile(code_out, code_in.at[tile], code_sem, tile_at(i), tile))
    code_in[tile] = code_out[...]

    side_half = jnp.where(lane < 64, 0.0, 1.0)
    for f in range(FINE):
        wanted = block_list[0, f]
        rank = jnp.max(jnp.where(lane == wanted, second, 0.0), axis=1, keepdims=True)
        select[f] = jnp.where(side_half == rank, wanted >> 3, -1)

    cells = obs_cells[...]
    cell_hot = jnp.where(
        lax.broadcasted_iota(I32, (CELLS, OBS), 0) == (cells & (CELLS - 1)), 1.0, 0.0
    ).astype(BF16)
    for i in range(2):
        cell_tall[i * CELLS : (i + 1) * CELLS, :] = cell_hot
        cell_wide[:, i * OBS : (i + 1) * OBS] = cell_hot

    def wait_code(i, carry):
        t = tile_at(i)
        to_tile(code_out, code_in.at[t], code_sem, t, t).wait_recv()
        return carry

    lax.fori_loop(1, TILES, wait_code, 0)
    lane3 = lane_of(TILES, 8, LANES)
    mine = (lane3 >> 3) == tile
    local = (lane3 & 7).astype(F32)
    codes = code_in[...]
    slot_0 = jnp.sum(jnp.where(mine & (codes == 1.0), local, 0.0), axis=2, keepdims=True)
    slot_1 = jnp.sum(jnp.where(mine & (codes == 2.0), local, 0.0), axis=2, keepdims=True)
    kept[...] = jnp.where(lane3 < 64, slot_0, slot_1)

    for copy in first_halo:
        copy.wait_recv()
    pl.semaphore_wait(news.at[0], 3)
    tell(1, two_off_mems)

    whole = with_halo(both, halo_in, tx, ty)
    field, rate = whole[:, :GROUPS], whole[:, GROUPS:]
    rates[...] = rate[:, 0]
    for sweep in range(SWEEPS):
        center = field[1:-1]
        beside = field[2:] + field[:-2] + turned(center, 1) + turned(center, -1)
        field = center + rate[1 + sweep : 23 - sweep] * (beside - 4.0 * center)

    field = jnp.where(lane < CYC, field, 0.0)
    field = (field + turned(field, 64)).reshape(2, CB, GROUPS, 8, LANES)
    for ky in range(CYC // CB):
        block = 0.0
        for x in range(CB):
            block = block + jnp.where(
                ((lane & 63) >> 3) == x, turned(field[:, x], CB * (x - ky)), 0.0
            )
        for kx in range(2):
            blocks[kx * (CYC // CB) + ky] = block[kx]

    def chosen(t):
        number = kept[t]
        block = jnp.zeros((GROUPS, 8, LANES), F32)
        for k in range(BLOCKS):
            block = jnp.where(number == float(k), blocks[k], block)
        return block

    for t in other_tiles:
        block_out[t] = chosen(t)
        to_tile(block_out.at[t], block_in.at[tile], block_sem, t, tile).start()
    sent.append(
        lambda i: to_tile(
            block_out.at[tile_at(i)], block_in.at[tile], block_sem, tile_at(i), tile
        )
    )
    block_in[tile] = chosen(tile)

    load_weights.wait()

    def split_weights(f, carry):
        high, low = halves(weights[f])
        split[f, 0:64] = high
        split[f, 64:128] = low
        return carry

    lax.fori_loop(0, FINE, split_weights, 0)
    load_perturb.wait()
    pl.semaphore_wait(news.at[1], 3)
    tell(2, [mem_by(0, 1)])

    pl.semaphore_wait(news.at[2], 1)
    observations[mem, 0:1, :] = departures[...]
    observations[mem, 1:2, :] = obs_weight[...]
    for m in other_mems:
        to_member(
            observations.at[mem], observations.at[mem], observed_sem, m, mem
        ).start()
    sent.append(
        lambda i: to_member(
            observations.at[mem], observations.at[mem], observed_sem, mem_at(i), mem
        )
    )

    def wait_blocks(i, carry):
        t = tile_at(i)
        to_tile(block_out.at[t], block_in.at[t], block_sem, t, t).wait_recv()
        return carry

    lax.fori_loop(1, TILES, wait_blocks, 0)

    for f in range(FINE):
        value = block_in[block_list[0, f] >> 3]
        value = jnp.where(select[f] >= 0, value, turned(value, 64))
        high, low = halves(value.reshape(ROWS, LANES))
        product = jnp.dot(
            jnp.concatenate([high, low], axis=0), split[f], preferred_element_type=F32
        )
        product = product[:ROWS] + product[ROWS:]
        fine_a[pl.ds(f, ROWS, stride=FINE), :] = product[:, :LANES]
        fine_b[pl.ds(f, ROWS, stride=FINE), :] = product[:, LANES:]

    def share(i, carry):
        level = i
        for half, fine in enumerate((fine_a, fine_b)):
            sums = [jnp.zeros((FINE, LANES), F32)] * VARS
            for m in range(ROWS // LEV):
                row = m * LEV + level
                value = fine[pl.ds(pl.multiple_of(row * FINE, FINE), FINE), :]
                for v in range(VARS):
                    part = perturb[row * VARS + v, :, half * LANES : (half + 1) * LANES]
                    sums[v] = sums[v] + value * part.astype(F32)
            for v in range(VARS):
                place = v % 2 * HALF + level * 2 + v // 2
                slab[place, :, half * LANES : (half + 1) * LANES] = sums[v]
        return carry

    lax.fori_loop(0, LEV, share, 0)

    fine_of = (cells >> 8) == lax.broadcasted_iota(I32, (FINE, OBS), 0)
    high, low = halves(slab[...].reshape(SLABS * FINE, CELLS))
    at_cells = jnp.dot(
        jnp.concatenate([high, low], axis=1), cell_tall[...], preferred_element_type=F32
    )
    for s in range(SLABS):
        place = s % 2 * HALF + s // 2
        here = at_cells[place * FINE : (place + 1) * FINE]
        seen_out[s // QUARTER, s % QUARTER : s % QUARTER + 1, :] = jnp.sum(
            jnp.where(fine_of, here, 0.0), axis=0, keepdims=True
        )

    quarter = lax.rem(mem, 4)
    z_twin = z + 1 - 2 * lax.rem(z, 2)
    square = [z_twin * 2 + (1 - run), z_twin * 2 + run, z * 2 + (1 - run)]
    in_square = [
        to_member_quarter(seen_out, seen_in, seen_sem, m, lax.rem(m, 4), quarter)
        for m in square
    ]
    for copy in in_square:
        copy.start()
    seen_in[quarter] = seen_out[quarter]
    for m in square:
        theirs = lax.rem(m, 4)
        to_member_quarter(seen_out, seen_in, seen_sem, m, theirs, theirs).wait_recv()
    partial[mem] = seen_in[0] + seen_in[1] + seen_in[2] + seen_in[3]
    for m in other_mems:
        to_member(partial.at[mem], partial.at[mem], partial_sem, m, mem).start()
    sent.append(
        lambda i: to_member(
            partial.at[mem], partial.at[mem], partial_sem, mem_at(i), mem
        )
    )

    def to_partner(i):
        first = (1 - run) * HALF + 2 * i
        return pltpu.make_async_remote_copy(
            src_ref=slab.at[pl.ds(first, 2)],
            dst_ref=paired_in.at[pl.ds(2 * i, 2)],
            send_sem=pair_sem.at[0, i],
            recv_sem=pair_sem.at[1, i],
            device_id={"mem": mem_by(0, 1)},
            device_id_type=MESH,
        )

    for i in range(HALF // 2):
        to_partner(i).start()

    def along_z(other, slot):
        return pltpu.make_async_remote_copy(
            src_ref=paired.at[other],
            dst_ref=slab_in.at[slot],
            send_sem=slab_sem.at[0, other],
            recv_sem=slab_sem.at[1, slot],
            device_id={"mem": other * 2 + run},
            device_id_type=MESH,
        )

    def z_at(i):
        return lax.rem(z + i, HALF)

    def wait_partial(i, carry):
        m = mem_at(i)
        to_member(
            observations.at[m], observations.at[m], observed_sem, m, m
        ).wait_recv()
        to_member(partial.at[m], partial.at[m], partial_sem, m, m).wait_recv()
        return carry

    lax.fori_loop(1, N_MEM, wait_partial, 0)

    in_use = lane_of(1, OBS) < obs_count[0, 0]
    for s in range(SLABS):
        at, row = s // QUARTER, slice(s % QUARTER, s % QUARTER + 1)
        seen = sum(partial[QUARTER * i + at, row, :] for i in range(4))
        residual = observations[s, 1:2, :] * (seen - observations[s, 0:1, :])
        weighted[s] = jnp.where(in_use, residual, 0.0)
    stores[1].start()

    for s in range(SLABS):
        high, low = halves(weighted[s])
        for i, part in enumerate((high, low)):
            spread[s * FINE : (s + 1) * FINE, i * OBS : (i + 1) * OBS] = jnp.where(
                fine_of, part.astype(F32), 0.0
            ).astype(BF16)
    forced = lax.dot_general(
        spread[...],
        cell_wide[...],
        (((1,), (1,)), ((), ())),
        preferred_element_type=F32,
    )
    forcing[...] = forced.reshape(SLABS, FINE, CELLS)

    def fine_gradient(level, carry):
        for half, fine in enumerate((fine_a, fine_b)):
            cut = slice(half * LANES, (half + 1) * LANES)
            parts = [forcing[level * VARS + v, :, cut] for v in range(VARS)]
            for m in range(ROWS // LEV):
                row = m * LEV + level
                value = sum(
                    perturb[row * VARS + v, :, cut].astype(F32) * parts[v]
                    for v in range(VARS)
                )
                fine[pl.ds(pl.multiple_of(row * FINE, FINE), FINE), :] = value
        return carry

    lax.fori_loop(0, LEV, fine_gradient, 0)

    for f in range(FINE):
        value = jnp.concatenate(
            [
                fine_a[pl.ds(f, ROWS, stride=FINE), :],
                fine_b[pl.ds(f, ROWS, stride=FINE), :],
            ],
            axis=1,
        )
        high, low = halves(value)
        product = lax.dot_general(
            jnp.concatenate([high, low], axis=0),
            split[f],
            (((1,), (1,)), ((), ())),
            preferred_element_type=F32,
        )
        product = product[:ROWS] + product[ROWS:]
        product = product + turned(product, 64)
        contrib[f] = product.reshape(GROUPS, 8, LANES)

    def returned(t):
        block = jnp.zeros((GROUPS, 8, LANES), F32)
        for f in range(FINE):
            block = block + jnp.where(select[f] == t, contrib[f], 0.0)
        return block

    for t in other_tiles:
        back_out[t] = returned(t)
        to_tile(back_out.at[t], back_in.at[tile], back_sem, t, tile).start()
    sent.append(
        lambda i: to_tile(
            back_out.at[tile_at(i)], back_in.at[tile], back_sem, tile_at(i), tile
        )
    )
    back_in[tile] = returned(tile)

    for i in range(HALF // 2):
        to_partner(i).wait_recv()
    paired[...] = slab[pl.ds(run * HALF, HALF)] + paired_in[...]
    for dz in (4, 3, 5, 2, 6, 1, 7):
        along_z(z_at(dz), z).start()

    def gather_back(t, blocks_so_far):
        number, given = kept[t], back_in[t]
        return tuple(
            block + jnp.where(number == float(k), given, 0.0)
            for k, block in enumerate(blocks_so_far)
        )

    def wait_back(i, blocks_so_far):
        t = tile_at(i)
        to_tile(back_out.at[t], back_in.at[t], back_sem, t, t).wait_recv()
        return gather_back(t, blocks_so_far)

    nothing = (jnp.zeros((GROUPS, 8, LANES), F32),) * BLOCKS
    gathered = lax.fori_loop(1, TILES, wait_back, gather_back(tile, nothing))
    for k, block in enumerate(gathered):
        blocks[k] = block + turned(block, 64)

    coarse = []
    for x in range(CXC):
        plane = 0.0
        for ky in range(CYC // CB):
            plane = plane + jnp.where(
                (lane >> 3) == ky,
                turned(blocks[x // CB * (CYC // CB) + ky], CB * (ky - x % CB)),
                0.0,
            )
        coarse.append(plane)
    for i, message in enumerate(packed_halo(coarse, ty)):
        edge_out[i] = message
    second_halo = halo_copies(edge_out, edge_in, edge_sem)
    for copy in second_halo:
        copy.start()

    def wait_sent(i, carry):
        for of_peer in sent:
            of_peer(i).wait_send()
        return carry

    lax.fori_loop(1, TILES, wait_sent, 0)
    for copy in first_halo + in_square:
        copy.wait_send()
    for copy in second_halo:
        copy.wait_recv()
    field = with_halo(coarse, edge_in, tx, ty)
    rate = rates[...][:, None]
    for sweep in range(SWEEPS):
        scaled = rate[sweep : 24 - sweep] * field
        inner = scaled[1:-1]
        beside = scaled[2:] + scaled[:-2] + turned(inner, 1) + turned(inner, -1)
        field = field[1:-1] + beside - 4.0 * inner
    field = field + planes[...]
    for x in range(CXC):
        rows[pl.ds(x, ROWS, stride=CXC), :] = field[x].reshape(ROWS, LANES)
    gradient[...] = rows[:, 0:CYC]
    stores[2].start()

    def gather_slab(i, total):
        other = z_at(i)
        along_z(other, other).wait_recv()
        return total + slab_in[other]

    increment[...] = lax.fori_loop(1, HALF, gather_slab, paired[z])
    stores[0].start()

    def wait_slab_sent(i, carry):
        along_z(z_at(i), z).wait_send()
        return carry

    lax.fori_loop(1, HALF, wait_slab_sent, 0)
    for i in range(HALF // 2):
        to_partner(i).wait_send()
    for copy in second_halo:
        copy.wait_send()
    for store in stores:
        store.wait()


def handed_on(*refs):
    sources, targets, held, load_sem, store_sem = (
        refs[:3],
        refs[3:6],
        refs[6:9],
        refs[9],
        refs[10],
    )
    loads = [
        pltpu.make_async_copy(source, here, load_sem.at[i])
        for i, (source, here) in enumerate(zip(sources, held))
    ]
    stores = [
        pltpu.make_async_copy(here, target, store_sem.at[i])
        for i, (here, target) in enumerate(zip(held, targets))
    ]
    for load in loads:
        load.start()
    for load, store in zip(loads, stores):
        load.wait()
        store.start()
    for store in stores:
        store.wait()


def on_device(
    alpha,
    filter_rate,
    block_list,
    interp_weights,
    perturbations,
    obs_cells,
    obs_count,
    departures,
    obs_weight,
):
    in_hbm = pl.BlockSpec(memory_space=pltpu.HBM)
    dma = pltpu.SemaphoreType.DMA
    results = (
        jax.ShapeDtypeStruct((FINE, CELLS), F32),
        jax.ShapeDtypeStruct((1, OBS), F32),
        jax.ShapeDtypeStruct((ROWS * CXC, CYC), F32),
    )
    made = pl.pallas_call(
        kernel,
        out_shape=results,
        in_specs=[in_hbm] * 9,
        out_specs=(in_hbm,) * 3,
        scratch_shapes=[
            pltpu.VMEM((FINE, CELLS), F32),
            pltpu.VMEM((ROWS * CXC, CYC), F32),
            pltpu.SMEM((1, FINE), I32),
            pltpu.SMEM((1, 1), I32),
            pltpu.VMEM((ROWS * CXC, CYC), F32),
            pltpu.VMEM((CXC, CYC), F32),
            pltpu.VMEM((1, OBS), I32),
            pltpu.VMEM((1, OBS), F32),
            pltpu.VMEM((1, OBS), F32),
            pltpu.VMEM((FINE, 64, CELLS), F32),
            pltpu.VMEM((ROWS * VARS, FINE, CELLS), BF16),
            pltpu.VMEM((FINE, 128, CELLS), BF16),
            pltpu.VMEM((ROWS * CXC, LANES), F32),
            pltpu.VMEM((CXC, GROUPS, 8, LANES), F32),
            pltpu.VMEM((CXC + 2 * SWEEPS, 8, LANES), F32),
            pltpu.VMEM((FINE, 8, LANES), I32),
            pltpu.VMEM((3, GROUPS + 1, 8, LANES), F32),
            pltpu.VMEM((5, GROUPS + 1, 8, LANES), F32),
            pltpu.VMEM((8, LANES), F32),
            pltpu.VMEM((TILES, 8, LANES), F32),
            pltpu.VMEM((TILES, 8, LANES), F32),
            pltpu.VMEM((BLOCKS, GROUPS, 8, LANES), F32),
            pltpu.VMEM((TILES, GROUPS, 8, LANES), F32),
            pltpu.VMEM((TILES, GROUPS, 8, LANES), F32),
            pltpu.VMEM((ROWS * FINE, LANES), F32),
            pltpu.VMEM((ROWS * FINE, LANES), F32),
            pltpu.VMEM((SLABS, FINE, CELLS), F32),
            pltpu.VMEM((HALF, FINE, CELLS), F32),
            pltpu.VMEM((HALF, FINE, CELLS), F32),
            pltpu.VMEM((HALF, FINE, CELLS), F32),
            pltpu.VMEM((SLABS, 1, OBS), F32),
            pltpu.VMEM((4, QUARTER, OBS), F32),
            pltpu.VMEM((4, QUARTER, OBS), F32),
            pltpu.VMEM((N_MEM, 2, OBS), F32),
            pltpu.VMEM((N_MEM, QUARTER, OBS), F32),
            pltpu.VMEM((2 * CELLS, OBS), BF16),
            pltpu.VMEM((CELLS, 2 * OBS), BF16),
            pltpu.VMEM((SLABS * FINE, 2 * OBS), BF16),
            pltpu.VMEM((SLABS, FINE, CELLS), F32),
            pltpu.VMEM((FINE, GROUPS, 8, LANES), F32),
            pltpu.VMEM((TILES, GROUPS, 8, LANES), F32),
            pltpu.VMEM((TILES, GROUPS, 8, LANES), F32),
            pltpu.VMEM((3, GROUPS, 8, LANES), F32),
            pltpu.VMEM((5, GROUPS, 8, LANES), F32),
            dma((9,)),
            dma((2, 5)),
            dma((2, TILES)),
            dma((2, TILES)),
            dma((2, HALF // 2)),
            dma((2, HALF)),
            dma((2, N_MEM)),
            dma((2, 4)),
            dma((2, N_MEM)),
            dma((2, TILES)),
            dma((2, 5)),
            pltpu.SemaphoreType.REGULAR((3,)),
            dma((3,)),
        ],
        compiler_params=pltpu.CompilerParams(
            collective_id=0, has_side_effects=True, vmem_limit_bytes=64 << 20
        ),
    )(
        block_list.reshape(1, FINE),
        obs_count.reshape(1, 1),
        alpha.reshape(ROWS * CXC, CYC),
        filter_rate,
        obs_cells.reshape(1, OBS),
        departures.reshape(1, OBS),
        obs_weight.reshape(1, OBS),
        interp_weights.reshape(FINE, 64, CELLS),
        perturbations.reshape(ROWS * VARS, FINE, CELLS),
    )
    increment, weighted, gradient = pl.pallas_call(
        handed_on,
        out_shape=results,
        in_specs=[in_hbm] * 3,
        out_specs=(in_hbm,) * 3,
        scratch_shapes=[pltpu.VMEM(r.shape, r.dtype) for r in results]
        + [dma((3,)), dma((3,))],
        compiler_params=pltpu.CompilerParams(vmem_limit_bytes=64 << 20),
    )(*made)
    return (
        increment.reshape(1, FINE, CELLS),
        weighted.reshape(departures.shape),
        gradient.reshape(alpha.shape),
    )


def solution(mesh):
    return jax.shard_map(
        on_device,
        mesh=mesh,
        in_specs=(
            P("mem", None, "tx", "ty"),
            P("tx", "ty"),
            P("tx", "ty", None),
            P("tx", "ty", None, None, None),
            P("mem", None, None, ("tx", "ty"), None),
            P("tx", "ty", None),
            P("tx", "ty"),
            P("tx", "ty", "mem", None),
            P("tx", "ty", "mem", None),
        ),
        out_specs=(
            P("mem", ("tx", "ty"), None),
            P("tx", "ty", "mem", None),
            P("mem", None, "tx", "ty"),
        ),
        check_vma=False,
    )
```

```python
import jax
import jax.numpy as jnp
from jax import lax
from jax.experimental import pallas as pl
from jax.experimental.pallas import tpu as pltpu
from jax.sharding import PartitionSpec as P

MESH = pl.DeviceIdType.MESH
F32, BF16, I32 = jnp.float32, jnp.bfloat16, jnp.int32

LEV = 4
VARS = 4
CB = 8
CXC = 16
CYC = 32
SWEEPS = 4
OBS = 512
ROWS = 32
GROUPS = ROWS // 8
FINE = 32
CELLS = 256
SLABS = 16
QUARTER = 4
HALF = 8
TILES = 16
N_MEM = 16
N_TX = 8
BLOCKS = 8
LANES = 128


def lane_of(*shape):
    return lax.broadcasted_iota(I32, shape, len(shape) - 1)


def turned(value, shift):
    if isinstance(shift, int):
        shift %= LANES
        if shift == 0:
            return value
    return pltpu.roll(value, shift, axis=value.ndim - 1)


def halves(value):
    high = value.astype(BF16)
    return high, (value - high.astype(F32)).astype(BF16)


def device_halo(tx, ty):
    below, above = lax.rem(tx + N_TX - 1, N_TX), lax.rem(tx + 1, N_TX)
    return ((below, ty), (above, ty), (below, 1 - ty), (above, 1 - ty), (tx, 1 - ty))


def packed_halo(planes, ty):
    lane = lane_of(8, LANES)
    first = sum(turned(planes[j], CYC * j) for j in range(SWEEPS))
    last = sum(turned(planes[CXC - SWEEPS + j], CYC * j) for j in range(SWEEPS))
    start = (CYC - SWEEPS) * (1 - ty)
    side = 0.0
    for x in range(CXC):
        shift = lax.rem(SWEEPS * x - start + LANES, LANES)
        side = side + jnp.where(lane >> 2 == x, turned(planes[x], shift), 0.0)
    return first, last, side


def with_halo(planes, halo, tx, ty):
    lane = lane_of(8, LANES)
    own = lane < CYC
    side = (lane >> 2) == jnp.where(ty == 0, CYC // 4, LANES // 4 - 1)
    corner = jnp.where(ty == 0, CYC, 3 * CYC)
    place = jnp.where(ty == 0, CYC, LANES - SWEEPS)

    def beyond(straight, across, there):
        made = []
        for j in range(SWEEPS):
            plane = jnp.where(own, turned(straight, -CYC * j), 0.0)
            shift = lax.rem(corner - CYC * j + LANES, LANES)
            plane = plane + jnp.where(side, turned(across, shift), 0.0)
            made.append(jnp.where(there, plane, 0.0))
        return made

    low = beyond(halo[1], halo[3], tx > 0)
    high = beyond(halo[0], halo[2], tx < N_TX - 1)
    middle = []
    for x in range(CXC):
        shift = lax.rem(place - SWEEPS * x + LANES, LANES)
        middle.append(planes[x] + jnp.where(side, turned(halo[4], shift), 0.0))
    return jnp.stack(low + middle + high)


def kernel(
    block_list_hbm,
    obs_count_hbm,
    alpha_hbm,
    filter_rate_hbm,
    obs_cells_hbm,
    departures_hbm,
    obs_weight_hbm,
    weights_hbm,
    perturb_hbm,
    increment_hbm,
    weighted_hbm,
    gradient_hbm,
    increment,
    gradient,
    block_list,
    obs_count,
    alpha,
    filter_rate,
    obs_cells,
    departures,
    obs_weight,
    weights,
    perturb,
    perturb_wide,
    split,
    rows,
    planes,
    rates,
    select,
    halo_out,
    halo_in,
    code_out,
    code_in,
    kept,
    blocks,
    block_out,
    block_in,
    fine_a,
    fine_b,
    slab,
    paired,
    paired_in,
    slab_in,
    weighted,
    seen_out,
    seen_in,
    observations,
    partial,
    cell_tall,
    cell_wide,
    spread,
    forcing,
    contrib,
    back_out,
    back_in,
    edge_out,
    edge_in,
    load_sem,
    halo_sem,
    code_sem,
    block_sem,
    pair_sem,
    slab_sem,
    observed_sem,
    seen_sem,
    partial_sem,
    back_sem,
    edge_sem,
    news,
    store_sem,
):
    mem, tx, ty = lax.axis_index("mem"), lax.axis_index("tx"), lax.axis_index("ty")
    tile = tx * 2 + ty
    lane = lane_of(8, LANES)
    sent = []

    loads = [
        pltpu.make_async_copy(source, target, load_sem.at[i])
        for i, (source, target) in enumerate(
            (
                (alpha_hbm, alpha),
                (filter_rate_hbm, filter_rate),
                (block_list_hbm, block_list),
                (obs_count_hbm, obs_count),
                (obs_cells_hbm, obs_cells),
                (departures_hbm, departures),
                (obs_weight_hbm, obs_weight),
                (weights_hbm, weights),
                (perturb_hbm, perturb),
            )
        )
    ]
    for load in loads:
        load.start()
    load_weights, load_perturb = loads[7:]
    stores = [
        pltpu.make_async_copy(source, target, store_sem.at[i])
        for i, (source, target) in enumerate(
            (
                (increment, increment_hbm),
                (weighted.at[lax.axis_index("mem")], weighted_hbm),
                (gradient, gradient_hbm),
            )
        )
    ]

    y, core = lax.div(tx, 2), lax.rem(tx, 2)
    z, run = lax.div(mem, 2), lax.rem(mem, 2)

    def tile_by(dy, dcore, dty):
        to_core = 1 - core if dcore else core
        return (lax.rem(y + dy, 4) * 2 + to_core) * 2 + (1 - ty if dty else ty)

    def mem_by(dz, drun):
        return lax.rem(z + dz, 8) * 2 + (1 - run if drun else run)

    other_tiles = [
        tile_by(dy, dcore, dty) for dty in (1, 0) for dy in (2, 1, 3, 0) for dcore in (1, 0)
    ][:-1]
    other_mems = [
        mem_by(dz, drun) for dz in (4, 3, 5, 2, 6, 1, 7, 0) for drun in (1, 0)
    ][:-1]

    def tile_at(i):
        return lax.rem(tile + i, TILES)

    def tile_device(t):
        return {"tx": lax.div(t, 2), "ty": lax.rem(t, 2)}

    def mem_at(i):
        return lax.rem(mem + i, N_MEM)

    beside_mems = [mem_by(1, 0), mem_by(7, 0), mem_by(0, 1)]
    two_off_mems = [mem_by(2, 0), mem_by(6, 0), mem_by(0, 1)]
    barrier = pltpu.get_barrier_semaphore()
    for t in other_tiles:
        pl.semaphore_signal(
            barrier, inc=1, device_id=tile_device(t), device_id_type=MESH
        )
    for m in beside_mems:
        pl.semaphore_signal(barrier, inc=1, device_id={"mem": m}, device_id_type=MESH)

    def tell(step, members):
        for m in members:
            pl.semaphore_signal(
                news.at[step], inc=1, device_id={"mem": m}, device_id_type=MESH
            )

    def to_tile(src, dst, sem, t, slot):
        return pltpu.make_async_remote_copy(
            src_ref=src,
            dst_ref=dst,
            send_sem=sem.at[0, t],
            recv_sem=sem.at[1, slot],
            device_id=tile_device(t),
            device_id_type=MESH,
        )

    def to_member(src, dst, sem, m, slot):
        return pltpu.make_async_remote_copy(
            src_ref=src,
            dst_ref=dst,
            send_sem=sem.at[0, m],
            recv_sem=sem.at[1, slot],
            device_id={"mem": m},
            device_id_type=MESH,
        )

    def to_member_quarter(src, dst, sem, m, theirs, mine):
        return pltpu.make_async_remote_copy(
            src_ref=src.at[theirs],
            dst_ref=dst.at[mine],
            send_sem=sem.at[0, theirs],
            recv_sem=sem.at[1, mine],
            device_id={"mem": m},
            device_id_type=MESH,
        )

    def halo_copies(out, into, sem):
        sources = (0, 1, 0, 1, 2)
        return [
            pltpu.make_async_remote_copy(
                src_ref=out.at[sources[i]],
                dst_ref=into.at[i],
                send_sem=sem.at[0, i],
                recv_sem=sem.at[1, i],
                device_id={"tx": x, "ty": y},
                device_id_type=MESH,
            )
            for i, (x, y) in enumerate(device_halo(tx, ty))
        ]

    rows[...] = jnp.zeros_like(rows)
    rates[...] = jnp.zeros_like(rates)
    for load in loads[:7]:
        load.wait()
    rows[:, 0:CYC] = alpha[...]
    for x in range(CXC):
        planes[x] = rows[pl.ds(x, ROWS, stride=CXC), :].reshape(GROUPS, 8, LANES)
        rates[SWEEPS + x, :, 0:CYC] = jnp.broadcast_to(
            filter_rate[x : x + 1, :], (8, CYC)
        )
    both = jnp.concatenate(
        [planes[...], rates[SWEEPS : SWEEPS + CXC][:, None]], axis=1
    )
    for i, message in enumerate(packed_halo(both, ty)):
        halo_out[i] = message

    asked = lane < 0
    for f in range(FINE):
        asked = asked | (lane == block_list[0, f])
    asked = jnp.where(asked, 1.0, 0.0)
    second = jnp.zeros((8, LANES), F32)
    for j in range(1, BLOCKS):
        second = jnp.maximum(second, jnp.where((lane & 7) >= j, turned(asked, j), 0.0))
    code_out[...] = asked * (1.0 + second)

    pl.semaphore_wait(barrier, TILES - 1 + 3)
    first_halo = halo_copies(halo_out, halo_in, halo_sem)
    for t in other_tiles[:6]:
        to_tile(code_out, code_in.at[tile], code_sem, t, tile).start()
    for copy in first_halo:
        copy.start()
    for t in other_tiles[6:]:
        to_tile(code_out, code_in.at[tile], code_sem, t, tile).start()
    tell(0, beside_mems)
    sent.append(lambda i: to_tile(code_out, code_in.at[tile], code_sem, tile_at(i), tile))
    code_in[tile] = code_out[...]

    side_half = jnp.where(lane < 64, 0.0, 1.0)
    for f in range(FINE):
        wanted = block_list[0, f]
        rank = jnp.max(jnp.where(lane == wanted, second, 0.0), axis=1, keepdims=True)
        select[f] = jnp.where(side_half == rank, wanted >> 3, -1)

    cells = obs_cells[...]
    cell_hot = jnp.where(
        lax.broadcasted_iota(I32, (CELLS, OBS), 0) == (cells & (CELLS - 1)), 1.0, 0.0
    ).astype(BF16)
    for i in range(2):
        cell_tall[i * CELLS : (i + 1) * CELLS, :] = cell_hot
        cell_wide[:, i * OBS : (i + 1) * OBS] = cell_hot

    def wait_code(i, carry):
        t = tile_at(i)
        to_tile(code_out, code_in.at[t], code_sem, t, t).wait_recv()
        return carry

    lax.fori_loop(1, TILES, wait_code, 0)
    lane3 = lane_of(TILES, 8, LANES)
    mine = (lane3 >> 3) == tile
    local = (lane3 & 7).astype(F32)
    codes = code_in[...]
    slot_0 = jnp.sum(jnp.where(mine & (codes == 1.0), local, 0.0), axis=2, keepdims=True)
    slot_1 = jnp.sum(jnp.where(mine & (codes == 2.0), local, 0.0), axis=2, keepdims=True)
    kept[...] = jnp.where(lane3 < 64, slot_0, slot_1)

    for copy in first_halo:
        copy.wait_recv()
    pl.semaphore_wait(news.at[0], 3)
    tell(1, two_off_mems)

    whole = with_halo(both, halo_in, tx, ty)
    field, rate = whole[:, :GROUPS], whole[:, GROUPS:]
    rates[...] = rate[:, 0]
    for sweep in range(SWEEPS):
        center = field[1:-1]
        beside = field[2:] + field[:-2] + turned(center, 1) + turned(center, -1)
        field = center + rate[1 + sweep : 23 - sweep] * (beside - 4.0 * center)

    field = jnp.where(lane < CYC, field, 0.0)
    field = (field + turned(field, 64)).reshape(2, CB, GROUPS, 8, LANES)
    for ky in range(CYC // CB):
        block = 0.0
        for x in range(CB):
            block = block + jnp.where(
                ((lane & 63) >> 3) == x, turned(field[:, x], CB * (x - ky)), 0.0
            )
        for kx in range(2):
            blocks[kx * (CYC // CB) + ky] = block[kx]

    def chosen(t):
        number = kept[t]
        block = jnp.zeros((GROUPS, 8, LANES), F32)
        for k in range(BLOCKS):
            block = jnp.where(number == float(k), blocks[k], block)
        return block

    for t in other_tiles:
        block_out[t] = chosen(t)
        to_tile(block_out.at[t], block_in.at[tile], block_sem, t, tile).start()
    sent.append(
        lambda i: to_tile(
            block_out.at[tile_at(i)], block_in.at[tile], block_sem, tile_at(i), tile
        )
    )
    block_in[tile] = chosen(tile)

    load_weights.wait()

    def split_weights(f, carry):
        high, low = halves(weights[f])
        split[f, 0:64] = high
        split[f, 64:128] = low
        return carry

    lax.fori_loop(0, FINE, split_weights, 0)
    load_perturb.wait()

    def widen(row, carry):
        cut = pl.ds(pl.multiple_of(row * 4, 4), 4)
        perturb_wide[cut] = perturb[cut].astype(F32)
        return carry

    lax.fori_loop(0, ROWS, widen, 0)
    pl.semaphore_wait(news.at[1], 3)
    tell(2, [mem_by(0, 1)])

    pl.semaphore_wait(news.at[2], 1)
    observations[mem, 0:1, :] = departures[...]
    observations[mem, 1:2, :] = obs_weight[...]
    for m in other_mems:
        to_member(
            observations.at[mem], observations.at[mem], observed_sem, m, mem
        ).start()
    sent.append(
        lambda i: to_member(
            observations.at[mem], observations.at[mem], observed_sem, mem_at(i), mem
        )
    )

    def wait_blocks(i, carry):
        t = tile_at(i)
        to_tile(block_out.at[t], block_in.at[t], block_sem, t, t).wait_recv()
        return carry

    lax.fori_loop(1, TILES, wait_blocks, 0)

    for f in range(FINE):
        value = block_in[block_list[0, f] >> 3]
        value = jnp.where(select[f] >= 0, value, turned(value, 64))
        high, low = halves(value.reshape(ROWS, LANES))
        product = jnp.dot(
            jnp.concatenate([high, low], axis=0), split[f], preferred_element_type=F32
        )
        product = product[:ROWS] + product[ROWS:]
        fine_a[pl.ds(f, ROWS, stride=FINE), :] = product[:, :LANES]
        fine_b[pl.ds(f, ROWS, stride=FINE), :] = product[:, LANES:]

    def share(i, carry):
        level = i
        for half, fine in enumerate((fine_a, fine_b)):
            sums = [jnp.zeros((FINE, LANES), F32)] * VARS
            for m in range(ROWS // LEV):
                row = m * LEV + level
                value = fine[pl.ds(pl.multiple_of(row * FINE, FINE), FINE), :]
                for v in range(VARS):
                    cut = slice(half * LANES, (half + 1) * LANES)
                    sums[v] = sums[v] + value * perturb_wide[row * VARS + v, :, cut]
            for v in range(VARS):
                place = v % 2 * HALF + level * 2 + v // 2
                slab[place, :, half * LANES : (half + 1) * LANES] = sums[v]
        return carry

    lax.fori_loop(0, LEV, share, 0)

    fine_of = (cells >> 8) == lax.broadcasted_iota(I32, (FINE, OBS), 0)
    high, low = halves(slab[...].reshape(SLABS * FINE, CELLS))
    at_cells = jnp.dot(
        jnp.concatenate([high, low], axis=1), cell_tall[...], preferred_element_type=F32
    )
    for s in range(SLABS):
        place = s % 2 * HALF + s // 2
        here = at_cells[place * FINE : (place + 1) * FINE]
        seen_out[s // QUARTER, s % QUARTER : s % QUARTER + 1, :] = jnp.sum(
            jnp.where(fine_of, here, 0.0), axis=0, keepdims=True
        )

    quarter = lax.rem(mem, 4)
    z_twin = z + 1 - 2 * lax.rem(z, 2)
    square = [z_twin * 2 + (1 - run), z_twin * 2 + run, z * 2 + (1 - run)]
    in_square = [
        to_member_quarter(seen_out, seen_in, seen_sem, m, lax.rem(m, 4), quarter)
        for m in square
    ]
    for copy in in_square:
        copy.start()
    seen_in[quarter] = seen_out[quarter]
    for m in square:
        theirs = lax.rem(m, 4)
        to_member_quarter(seen_out, seen_in, seen_sem, m, theirs, theirs).wait_recv()
    partial[mem] = seen_in[0] + seen_in[1] + seen_in[2] + seen_in[3]
    for m in other_mems:
        to_member(partial.at[mem], partial.at[mem], partial_sem, m, mem).start()
    sent.append(
        lambda i: to_member(
            partial.at[mem], partial.at[mem], partial_sem, mem_at(i), mem
        )
    )

    def to_partner(i):
        first = (1 - run) * HALF + 2 * i
        return pltpu.make_async_remote_copy(
            src_ref=slab.at[pl.ds(first, 2)],
            dst_ref=paired_in.at[pl.ds(2 * i, 2)],
            send_sem=pair_sem.at[0, i],
            recv_sem=pair_sem.at[1, i],
            device_id={"mem": mem_by(0, 1)},
            device_id_type=MESH,
        )

    for i in range(HALF // 2):
        to_partner(i).start()

    def along_z(other, slot):
        return pltpu.make_async_remote_copy(
            src_ref=paired.at[other],
            dst_ref=slab_in.at[slot],
            send_sem=slab_sem.at[0, other],
            recv_sem=slab_sem.at[1, slot],
            device_id={"mem": other * 2 + run},
            device_id_type=MESH,
        )

    def z_at(i):
        return lax.rem(z + i, HALF)

    def wait_partial(i, carry):
        m = mem_at(i)
        to_member(
            observations.at[m], observations.at[m], observed_sem, m, m
        ).wait_recv()
        to_member(partial.at[m], partial.at[m], partial_sem, m, m).wait_recv()
        return carry

    lax.fori_loop(1, N_MEM, wait_partial, 0)

    in_use = lane_of(1, OBS) < obs_count[0, 0]
    for s in range(SLABS):
        at, row = s // QUARTER, slice(s % QUARTER, s % QUARTER + 1)
        seen = sum(partial[QUARTER * i + at, row, :] for i in range(4))
        residual = observations[s, 1:2, :] * (seen - observations[s, 0:1, :])
        weighted[s] = jnp.where(in_use, residual, 0.0)
    stores[1].start()

    for s in range(SLABS):
        high, low = halves(weighted[s])
        for i, part in enumerate((high, low)):
            spread[s * FINE : (s + 1) * FINE, i * OBS : (i + 1) * OBS] = jnp.where(
                fine_of, part.astype(F32), 0.0
            ).astype(BF16)
    forced = lax.dot_general(
        spread[...],
        cell_wide[...],
        (((1,), (1,)), ((), ())),
        preferred_element_type=F32,
    )
    forcing[...] = forced.reshape(SLABS, FINE, CELLS)

    def fine_gradient(level, carry):
        for half, fine in enumerate((fine_a, fine_b)):
            cut = slice(half * LANES, (half + 1) * LANES)
            parts = [forcing[level * VARS + v, :, cut] for v in range(VARS)]
            for m in range(ROWS // LEV):
                row = m * LEV + level
                value = sum(
                    perturb_wide[row * VARS + v, :, cut] * parts[v]
                    for v in range(VARS)
                )
                fine[pl.ds(pl.multiple_of(row * FINE, FINE), FINE), :] = value
        return carry

    lax.fori_loop(0, LEV, fine_gradient, 0)

    for f in range(FINE):
        value = jnp.concatenate(
            [
                fine_a[pl.ds(f, ROWS, stride=FINE), :],
                fine_b[pl.ds(f, ROWS, stride=FINE), :],
            ],
            axis=1,
        )
        high, low = halves(value)
        product = lax.dot_general(
            jnp.concatenate([high, low], axis=0),
            split[f],
            (((1,), (1,)), ((), ())),
            preferred_element_type=F32,
        )
        product = product[:ROWS] + product[ROWS:]
        product = product + turned(product, 64)
        contrib[f] = product.reshape(GROUPS, 8, LANES)

    def returned(t):
        block = jnp.zeros((GROUPS, 8, LANES), F32)
        for f in range(FINE):
            block = block + jnp.where(select[f] == t, contrib[f], 0.0)
        return block

    for t in other_tiles:
        back_out[t] = returned(t)
        to_tile(back_out.at[t], back_in.at[tile], back_sem, t, tile).start()
    sent.append(
        lambda i: to_tile(
            back_out.at[tile_at(i)], back_in.at[tile], back_sem, tile_at(i), tile
        )
    )
    back_in[tile] = returned(tile)

    for i in range(HALF // 2):
        to_partner(i).wait_recv()
    paired[...] = slab[pl.ds(run * HALF, HALF)] + paired_in[...]
    for dz in (4, 3, 5, 2, 6, 1, 7):
        along_z(z_at(dz), z).start()

    def gather_back(t, blocks_so_far):
        number, given = kept[t], back_in[t]
        return tuple(
            block + jnp.where(number == float(k), given, 0.0)
            for k, block in enumerate(blocks_so_far)
        )

    def wait_back(i, blocks_so_far):
        t = tile_at(i)
        to_tile(back_out.at[t], back_in.at[t], back_sem, t, t).wait_recv()
        return gather_back(t, blocks_so_far)

    nothing = (jnp.zeros((GROUPS, 8, LANES), F32),) * BLOCKS
    gathered = lax.fori_loop(1, TILES, wait_back, gather_back(tile, nothing))
    for k, block in enumerate(gathered):
        blocks[k] = block + turned(block, 64)

    coarse = []
    for x in range(CXC):
        plane = 0.0
        for ky in range(CYC // CB):
            plane = plane + jnp.where(
                (lane >> 3) == ky,
                turned(blocks[x // CB * (CYC // CB) + ky], CB * (ky - x % CB)),
                0.0,
            )
        coarse.append(plane)
    for i, message in enumerate(packed_halo(coarse, ty)):
        edge_out[i] = message
    second_halo = halo_copies(edge_out, edge_in, edge_sem)
    for copy in second_halo:
        copy.start()

    def wait_sent(i, carry):
        for of_peer in sent:
            of_peer(i).wait_send()
        return carry

    lax.fori_loop(1, TILES, wait_sent, 0)
    for copy in first_halo + in_square:
        copy.wait_send()
    for copy in second_halo:
        copy.wait_recv()
    field = with_halo(coarse, edge_in, tx, ty)
    rate = rates[...][:, None]
    for sweep in range(SWEEPS):
        scaled = rate[sweep : 24 - sweep] * field
        inner = scaled[1:-1]
        beside = scaled[2:] + scaled[:-2] + turned(inner, 1) + turned(inner, -1)
        field = field[1:-1] + beside - 4.0 * inner
    field = field + planes[...]
    for x in range(CXC):
        rows[pl.ds(x, ROWS, stride=CXC), :] = field[x].reshape(ROWS, LANES)
    gradient[...] = rows[:, 0:CYC]
    stores[2].start()

    def gather_slab(i, total):
        other = z_at(i)
        along_z(other, other).wait_recv()
        return total + slab_in[other]

    increment[...] = lax.fori_loop(1, HALF, gather_slab, paired[z])
    stores[0].start()

    def wait_slab_sent(i, carry):
        along_z(z_at(i), z).wait_send()
        return carry

    lax.fori_loop(1, HALF, wait_slab_sent, 0)
    for i in range(HALF // 2):
        to_partner(i).wait_send()
    for copy in second_halo:
        copy.wait_send()
    for store in stores:
        store.wait()


def handed_on(*refs):
    sources, targets, held, load_sem, store_sem = (
        refs[:3],
        refs[3:6],
        refs[6:9],
        refs[9],
        refs[10],
    )
    loads = [
        pltpu.make_async_copy(source, here, load_sem.at[i])
        for i, (source, here) in enumerate(zip(sources, held))
    ]
    stores = [
        pltpu.make_async_copy(here, target, store_sem.at[i])
        for i, (here, target) in enumerate(zip(held, targets))
    ]
    for load in loads:
        load.start()
    for load, store in zip(loads, stores):
        load.wait()
        store.start()
    for store in stores:
        store.wait()


def on_device(
    alpha,
    filter_rate,
    block_list,
    interp_weights,
    perturbations,
    obs_cells,
    obs_count,
    departures,
    obs_weight,
):
    in_hbm = pl.BlockSpec(memory_space=pltpu.HBM)
    dma = pltpu.SemaphoreType.DMA
    results = (
        jax.ShapeDtypeStruct((FINE, CELLS), F32),
        jax.ShapeDtypeStruct((1, OBS), F32),
        jax.ShapeDtypeStruct((ROWS * CXC, CYC), F32),
    )
    made = pl.pallas_call(
        kernel,
        out_shape=results,
        in_specs=[in_hbm] * 9,
        out_specs=(in_hbm,) * 3,
        scratch_shapes=[
            pltpu.VMEM((FINE, CELLS), F32),
            pltpu.VMEM((ROWS * CXC, CYC), F32),
            pltpu.SMEM((1, FINE), I32),
            pltpu.SMEM((1, 1), I32),
            pltpu.VMEM((ROWS * CXC, CYC), F32),
            pltpu.VMEM((CXC, CYC), F32),
            pltpu.VMEM((1, OBS), I32),
            pltpu.VMEM((1, OBS), F32),
            pltpu.VMEM((1, OBS), F32),
            pltpu.VMEM((FINE, 64, CELLS), F32),
            pltpu.VMEM((ROWS * VARS, FINE, CELLS), BF16),
            pltpu.VMEM((ROWS * VARS, FINE, CELLS), F32),
            pltpu.VMEM((FINE, 128, CELLS), BF16),
            pltpu.VMEM((ROWS * CXC, LANES), F32),
            pltpu.VMEM((CXC, GROUPS, 8, LANES), F32),
            pltpu.VMEM((CXC + 2 * SWEEPS, 8, LANES), F32),
            pltpu.VMEM((FINE, 8, LANES), I32),
            pltpu.VMEM((3, GROUPS + 1, 8, LANES), F32),
            pltpu.VMEM((5, GROUPS + 1, 8, LANES), F32),
            pltpu.VMEM((8, LANES), F32),
            pltpu.VMEM((TILES, 8, LANES), F32),
            pltpu.VMEM((TILES, 8, LANES), F32),
            pltpu.VMEM((BLOCKS, GROUPS, 8, LANES), F32),
            pltpu.VMEM((TILES, GROUPS, 8, LANES), F32),
            pltpu.VMEM((TILES, GROUPS, 8, LANES), F32),
            pltpu.VMEM((ROWS * FINE, LANES), F32),
            pltpu.VMEM((ROWS * FINE, LANES), F32),
            pltpu.VMEM((SLABS, FINE, CELLS), F32),
            pltpu.VMEM((HALF, FINE, CELLS), F32),
            pltpu.VMEM((HALF, FINE, CELLS), F32),
            pltpu.VMEM((HALF, FINE, CELLS), F32),
            pltpu.VMEM((SLABS, 1, OBS), F32),
            pltpu.VMEM((4, QUARTER, OBS), F32),
            pltpu.VMEM((4, QUARTER, OBS), F32),
            pltpu.VMEM((N_MEM, 2, OBS), F32),
            pltpu.VMEM((N_MEM, QUARTER, OBS), F32),
            pltpu.VMEM((2 * CELLS, OBS), BF16),
            pltpu.VMEM((CELLS, 2 * OBS), BF16),
            pltpu.VMEM((SLABS * FINE, 2 * OBS), BF16),
            pltpu.VMEM((SLABS, FINE, CELLS), F32),
            pltpu.VMEM((FINE, GROUPS, 8, LANES), F32),
            pltpu.VMEM((TILES, GROUPS, 8, LANES), F32),
            pltpu.VMEM((TILES, GROUPS, 8, LANES), F32),
            pltpu.VMEM((3, GROUPS, 8, LANES), F32),
            pltpu.VMEM((5, GROUPS, 8, LANES), F32),
            dma((9,)),
            dma((2, 5)),
            dma((2, TILES)),
            dma((2, TILES)),
            dma((2, HALF // 2)),
            dma((2, HALF)),
            dma((2, N_MEM)),
            dma((2, 4)),
            dma((2, N_MEM)),
            dma((2, TILES)),
            dma((2, 5)),
            pltpu.SemaphoreType.REGULAR((3,)),
            dma((3,)),
        ],
        compiler_params=pltpu.CompilerParams(
            collective_id=0, has_side_effects=True, vmem_limit_bytes=64 << 20
        ),
    )(
        block_list.reshape(1, FINE),
        obs_count.reshape(1, 1),
        alpha.reshape(ROWS * CXC, CYC),
        filter_rate,
        obs_cells.reshape(1, OBS),
        departures.reshape(1, OBS),
        obs_weight.reshape(1, OBS),
        interp_weights.reshape(FINE, 64, CELLS),
        perturbations.reshape(ROWS * VARS, FINE, CELLS),
    )
    increment, weighted, gradient = pl.pallas_call(
        handed_on,
        out_shape=results,
        in_specs=[in_hbm] * 3,
        out_specs=(in_hbm,) * 3,
        scratch_shapes=[pltpu.VMEM(r.shape, r.dtype) for r in results]
        + [dma((3,)), dma((3,))],
        compiler_params=pltpu.CompilerParams(vmem_limit_bytes=64 << 20),
    )(*made)
    return (
        increment.reshape(1, FINE, CELLS),
        weighted.reshape(departures.shape),
        gradient.reshape(alpha.shape),
    )


def solution(mesh):
    return jax.shard_map(
        on_device,
        mesh=mesh,
        in_specs=(
            P("mem", None, "tx", "ty"),
            P("tx", "ty"),
            P("tx", "ty", None),
            P("tx", "ty", None, None, None),
            P("mem", None, None, ("tx", "ty"), None),
            P("tx", "ty", None),
            P("tx", "ty"),
            P("tx", "ty", "mem", None),
            P("tx", "ty", "mem", None),
        ),
        out_specs=(
            P("mem", ("tx", "ty"), None),
            P("tx", "ty", "mem", None),
            P("mem", None, "tx", "ty"),
        ),
        check_vma=False,
    )
```
